32 devices in a mesh: seq: 16 (over z, x, core), tp: 2 (over y).
Axes of the slice: x: 2, y: 2, z: 4, core: 2. Of those that a mesh axis runs over, the one named last changes fastest.
Arguments:
- values: bfloat16 [4096, 4096], P('seq', 'tp'), may hold values from -6 to 6
- gate: bfloat16 [4096, 4096], P('seq', 'tp'), may hold values from -6 to 6
- out_grad: bfloat16 [4096, 4096], P('seq', 'tp'), may hold values from -6 to 6
- out_weight: bfloat16 [4096, 4096], P(None, 'tp'), may hold values from -0.09375 to 0.09375
- filt: float32 [4096, 4096], P('seq', 'tp'), may hold values from -6 to 6
- decay: float32 [4096], P('tp'), may hold values from 0.5 to 16
Outputs:
- d_values: bfloat16 [4096, 4096], P('seq', 'tp')
- d_gate: bfloat16 [4096, 4096], P('seq', 'tp')
- d_filt: float32 [4096, 4096], P('seq', 'tp')
- decay_grad: float32 [4096], P('tp')
- d_out_weight: float32 [4096, 4096], P('seq', 'tp')
The draws below stay inside these ranges and needn't reach their ends.
All inputs are finite; a program needn't handle non-finite values.
Results may differ from the reference program's by a relative error of at most 0.0085.
Values may be sent and summed in bfloat16 or wider, within the bound.
No kernel may reach another device: no remote copies, remote signals or barrier semaphores. Data moves between devices by JAX's collectives and lax.ppermute only.
A program may use at most 192 MiB of HBM per device.

```python
import math
import jax
import jax.numpy as jnp
from jax import lax

D = 4096
TOKENS = 4096


def with_spikes(values, rng, source, target, shards_of, factor):
    def block_of(axis_at):
        return (jnp.arange(values.shape[axis_at]) // (values.shape[axis_at] // shards_of)).reshape((-1,) + (1,) * (values.ndim - 1 - axis_at))

    first = jax.random.permutation(rng, shards_of)[block_of(target)]
    other_side = (block_of(target) + shards_of // 2) % shards_of
    return jnp.where((block_of(source) == first) | (block_of(source) == other_side), factor * values, values)


def block_levels(rng, dims, shards, least, largest):
    level = 1.0
    for dim, shards_of in shards:
        heights = jax.random.uniform(jax.random.fold_in(jax.random.fold_in(rng, 6), dim), (shards_of,), jnp.float32, least / len(shards), largest / len(shards))
        level = level * jnp.repeat(jnp.exp(heights), dims[dim] // shards_of).reshape((-1,) + (1,) * (len(dims) - 1 - dim))
    return level


def centred(rng, dims, scale, bound, pieces=(), kind=jnp.bfloat16):
    factor_of = block_levels(rng, dims, pieces, -0.22, 0.18) if pieces else 1.0
    drawn = jax.random.normal(rng, dims, jnp.float32) * scale * factor_of
    return jnp.minimum(jnp.maximum(drawn, -bound), bound).astype(kind)


def noise_with(key, dims, spread, most, shards, heavy, kind=jnp.bfloat16):
    drawn = spread * jax.random.normal(key, dims, jnp.float32)
    if shards:
        drawn = drawn * block_levels(key, dims, shards, -0.22, 0.18)
    return jnp.clip(with_spikes(drawn, jax.random.fold_in(key, 3), *heavy), -most, most).astype(kind)


def setup_inputs(seed: int = 0) -> dict:
    seeds = jax.random.split(jax.random.key(seed), 7)
    return {
        "values": centred(seeds[0], (TOKENS, D), 1.0, 6.0, ((0, 16), (1, 2))),
        "gate": centred(seeds[1], (TOKENS, D), 1.0, 6.0, ((0, 16), (1, 2))),
        "out_grad": noise_with(seeds[2], (TOKENS, D), 1.0, 6.0, ((0, 16), (1, 2)), (0, 1, 16, 2.0)),
        "out_weight": centred(seeds[3], (D, D), D ** -0.5, 0.09375, ((1, 2),)),
        "filt": centred(seeds[4], (TOKENS, D), 1.0, 6.0, ((0, 16), (1, 2)), jnp.float32),
        "decay": jnp.clip(jnp.exp(math.log(16.0) - 3.465736 * jax.random.uniform(seeds[5], (D,), jnp.float32) ** block_levels(seeds[5], (D,), ((0, 2),), -0.2, 0.2)), 0.5, 16.0),
    }


def conv_block(inputs):
    values_blk, kernel_blk, grad_blk = inputs
    count = values_blk.shape[0]
    padded = 2 * count
    spec_v = jnp.fft.rfft(values_blk, n=padded, axis=0)
    spec_k = jnp.fft.rfft(kernel_blk, n=padded, axis=0)
    spec_g = jnp.fft.rfft(grad_blk, n=padded, axis=0)
    conv_out = jnp.fft.irfft(spec_v * spec_k, n=padded, axis=0)[:count]
    conv_grad = jnp.fft.irfft(jnp.conj(spec_k) * spec_g, n=padded, axis=0)[:count]
    kernel_grad = jnp.fft.irfft(jnp.conj(spec_v) * spec_g, n=padded, axis=0)[:count]
    return (conv_out, conv_grad, kernel_grad)

def reference(values, gate, out_grad, out_weight, filt, decay):
    grad_y = jnp.dot(out_grad, out_weight, preferred_element_type=jnp.float32).astype(jnp.bfloat16)
    position = (jnp.arange(TOKENS, dtype=jnp.int32).astype(jnp.float32) / TOKENS)[:, None]
    norm_scale = 1.0 / math.sqrt(TOKENS)
    window = jnp.exp(-decay[None, :] * position)
    kernel = filt * window * norm_scale
    gated_grad = grad_y.astype(jnp.float32) * gate.astype(jnp.float32)
    block_width = math.gcd(D, 512)
    blocks = D // block_width

    def split_up(array):
        return array.reshape(TOKENS, blocks, block_width).transpose(1, 0, 2)

    def join_up(array):
        return array.transpose(1, 0, 2).reshape(TOKENS, D)
    conv_out, conv_grad, kernel_grad = lax.map(conv_block, (split_up(values.astype(jnp.float32)), split_up(kernel), split_up(gated_grad)))
    conv_out = join_up(conv_out)
    conv_grad = join_up(conv_grad)
    kernel_grad = join_up(kernel_grad)
    d_values = conv_grad.astype(jnp.bfloat16)
    d_gate = (grad_y.astype(jnp.float32) * conv_out).astype(jnp.bfloat16)
    d_filt = kernel_grad * window * norm_scale
    decay_grad = -norm_scale * lax.optimization_barrier(jnp.sum(position * kernel_grad * kernel, axis=0))
    gated_out = (gate.astype(jnp.float32) * conv_out).astype(jnp.bfloat16)
    d_out_weight = jnp.dot(out_grad.T, gated_out, preferred_element_type=jnp.float32) * norm_scale
    return (d_values, d_gate, d_filt, decay_grad, d_out_weight)
```

```python
import math

import jax
import jax.numpy as jnp
import ml_dtypes
import numpy as np
from jax import lax
from jax.sharding import PartitionSpec as P

BF16 = jnp.bfloat16
F32 = jnp.float32
RADIX = 128


def split_bf16(array):
    high = array.astype(ml_dtypes.bfloat16)
    low = (array - high.astype(np.float64)).astype(ml_dtypes.bfloat16)
    return (high, low)


def transform_tables(length):
    padded = 2 * length
    outer = padded // RADIX
    half = outer // 2
    k1 = np.arange(half + 1)
    p = np.arange(half)
    r = np.arange(RADIX)
    phase = 2.0 * np.pi * (np.outer(k1, p) % outer) / outer
    first = np.stack([np.cos(phase), -np.sin(phase)], axis=1).reshape(2 * (half + 1), half)
    weight = np.full(half + 1, 2.0)
    weight[0] = weight[-1] = 1.0
    last = np.stack(
        [np.cos(phase) * weight[:, None], -np.sin(phase) * weight[:, None]], axis=1
    ).reshape(2 * (half + 1), half)
    inner = k1[:, None, None] * r[None, None, :] + outer * (r[:, None] * r[None, :])[None]
    inner_phase = 2.0 * np.pi * (inner % padded) / padded
    cos, sin = np.cos(inner_phase), np.sin(inner_phase)
    middle = np.concatenate(
        [np.concatenate([cos, sin], axis=2), np.concatenate([-sin, cos], axis=2)], axis=1
    )
    return first, middle, last.T / padded


def forward(block, first, middle):
    half, radix, channels = block.shape
    mid = sum(
        jnp.einsum("kp,prc->krc", part, block, preferred_element_type=F32) for part in first
    ).astype(BF16)
    mid = mid.reshape(half + 1, 2 * radix, channels)
    spec = jnp.einsum("kab,kbc->kac", middle, mid, preferred_element_type=F32)
    return spec.reshape(half + 1, 2, radix, channels)


def backward(spec, middle, last):
    count, _, radix, channels = spec.shape
    mid = jnp.einsum(
        "kba,kbc->kac",
        middle,
        spec.reshape(count, 2 * radix, channels).astype(BF16),
        preferred_element_type=F32,
    ).astype(BF16)
    mid = mid.reshape(2 * count, radix, channels)
    return sum(
        jnp.einsum("pk,krc->prc", part, mid, preferred_element_type=F32) for part in last
    )


def times(a, b):
    return jnp.stack(
        [a[:, 0] * b[:, 0] - a[:, 1] * b[:, 1], a[:, 0] * b[:, 1] + a[:, 1] * b[:, 0]], axis=1
    )


def conj_times(a, b):
    return jnp.stack(
        [a[:, 0] * b[:, 0] + a[:, 1] * b[:, 1], a[:, 0] * b[:, 1] - a[:, 1] * b[:, 0]], axis=1
    )


def swap(array, axis, size, bit):
    return lax.ppermute(array, axis, [(i, i ^ bit) for i in range(size)])


def gather_columns(block, axis):
    size = lax.axis_size(axis)
    if size != 2:
        return lax.all_gather(block, axis, axis=1, tiled=True)
    other = swap(block, axis, size, 1)
    first = lax.axis_index(axis) == 0
    return jnp.concatenate(
        [jnp.where(first, block, other), jnp.where(first, other, block)], axis=1
    )


def line_reduce_scatter(parts, size, inner):
    outer = size // inner
    z = lax.axis_index("seq") // inner
    total = lax.dynamic_index_in_dim(parts, z, 0, keepdims=False).astype(F32)
    right = left = None
    for step in range(1, outer):
        ahead = lax.dynamic_index_in_dim(
            parts, jnp.minimum(z + outer - step, outer - 1), 0, keepdims=False
        )
        behind = lax.dynamic_index_in_dim(
            parts, jnp.maximum(z - outer + step, 0), 0, keepdims=False
        )
        if right is not None:
            ahead = (ahead.astype(F32) + right.astype(F32)).astype(BF16)
            behind = (behind.astype(F32) + left.astype(F32)).astype(BF16)
        to_right = [(i, i + inner) for i in range(size) if i // inner < step]
        to_left = [(i, i - inner) for i in range(size) if i // inner >= outer - step]
        right = lax.ppermute(ahead, "seq", to_right)
        left = lax.ppermute(behind, "seq", to_left)
    if right is not None:
        total = total + right.astype(F32) + left.astype(F32)
    return total


def on_device(values, gate, out_grad, out_weight, filt, decay):
    rows, width = values.shape
    seq = lax.axis_size("seq")
    me = lax.axis_index("seq")
    length = rows * seq
    own = width // seq
    norm_scale = 1.0 / math.sqrt(length)
    inner = 4 if seq % 4 == 0 else 1
    outer = seq // inner
    first, middle, last = transform_tables(length)
    first = [jnp.asarray(part) for part in split_bf16(first)]
    last = [jnp.asarray(part) for part in split_bf16(last)]
    middle = jnp.asarray(middle.astype(ml_dtypes.bfloat16))
    half = length // RADIX

    def to_channels(block):
        parts = block.astype(BF16).reshape(rows, seq, own).transpose(1, 0, 2)
        moved = lax.all_to_all(parts, "seq", split_axis=0, concat_axis=0, tiled=True)
        return moved.reshape(half, RADIX, own)

    def to_tokens(block):
        moved = lax.all_to_all(block, "seq", split_axis=0, concat_axis=0, tiled=True)
        return moved.transpose(1, 0, 2).reshape(-1, width)

    full_grad = gather_columns(out_grad, "tp")
    grad_y = jnp.dot(full_grad, out_weight, preferred_element_type=F32).astype(BF16)

    position = ((me * rows + jnp.arange(rows, dtype=jnp.int32)).astype(F32) / length)[:, None]
    window = jnp.exp(-decay[None, :] * position)
    kernel = filt * window * norm_scale
    gated_grad = grad_y.astype(F32) * gate.astype(F32)

    values_c = to_channels(values)
    kernel_c = to_channels(kernel)
    grad_c = to_channels(gated_grad)
    spec_v = forward(values_c, first, middle)
    spec_k = forward(kernel_c, first, middle)
    conv_out_c = backward(times(spec_v, spec_k), middle, last).astype(BF16)
    conv_out = to_tokens(conv_out_c.reshape(seq, rows, own)).astype(F32)
    spec_g = forward(grad_c, first, middle)
    kernel_grad_c = backward(conj_times(spec_v, spec_g), middle, last)
    place = (jnp.arange(length, dtype=jnp.int32).astype(F32) / length).reshape(half, RADIX, 1)
    decay_part = -norm_scale * jnp.sum(
        place * kernel_grad_c * kernel_c.astype(F32), axis=(0, 1)
    )
    decay_high = decay_part.astype(BF16)
    decay_low = (decay_part - decay_high.astype(F32)).astype(BF16)
    extra = jnp.concatenate(
        [decay_high[None], decay_low[None], jnp.zeros((14, own), BF16)], axis=0
    )
    sent = jnp.concatenate(
        [
            kernel_grad_c.astype(BF16).reshape(seq, rows, own),
            jnp.broadcast_to(extra[None], (seq, 16, own)),
        ],
        axis=1,
    )
    returned = to_tokens(sent).astype(F32)
    kernel_grad = returned[:rows]
    decay_grad = returned[rows] + returned[rows + 1]
    conv_grad_c = backward(conj_times(spec_k, spec_g), middle, last).astype(BF16)
    d_values = to_tokens(conv_grad_c.reshape(seq, rows, own))

    d_gate = (grad_y.astype(F32) * conv_out).astype(BF16)
    gated_out = (gate.astype(F32) * conv_out).astype(BF16)
    d_filt = kernel_grad * window * norm_scale

    features = full_grad.shape[1] // seq
    by_inner = full_grad.reshape(rows, outer, inner, features)
    grads = []
    outs = [gated_out]
    for bit in range(inner):
        target = (me % inner) ^ bit
        piece = lax.dynamic_index_in_dim(by_inner, target, 2, keepdims=False)
        piece = piece.reshape(rows, outer * features)
        grads.append(swap(piece, "seq", seq, bit) if bit else piece)
    bit = 1
    while bit < inner:
        outs = outs + [swap(part, "seq", seq, bit) for part in outs]
        bit *= 2
    terms = lax.dot_general(
        jnp.concatenate(grads, axis=0),
        jnp.concatenate(outs, axis=0),
        (((0,), (0,)), ((), ())),
        preferred_element_type=F32,
    ).astype(BF16)
    terms = terms.reshape(outer, features, width)
    d_out_weight = line_reduce_scatter(terms, seq, inner) * norm_scale
    return (d_values, d_gate, d_filt, decay_grad, d_out_weight)


def solution(mesh):
    in_specs = (
        P("seq", "tp"),
        P("seq", "tp"),
        P("seq", "tp"),
        P(None, "tp"),
        P("seq", "tp"),
        P("tp"),
    )
    out_specs = (P("seq", "tp"), P("seq", "tp"), P("seq", "tp"), P("tp"), P("seq", "tp"))
    return jax.shard_map(
        on_device, mesh=mesh, in_specs=in_specs, out_specs=out_specs, check_vma=False
    )
```

```python
import functools
import math

import jax
import jax.numpy as jnp
import ml_dtypes
import numpy as np
from jax import lax
from jax.experimental import pallas as pl
from jax.experimental.pallas import tpu as pltpu
from jax.sharding import PartitionSpec as P

BF16 = jnp.bfloat16
F32 = jnp.float32
RADIX = 128
STEP = 16
VMEM_BYTES = 48 * 1024 * 1024


def middle_tables(length):
    padded = 2 * length
    outer = padded // RADIX
    k1 = np.arange(outer // 2 + 1)
    r = np.arange(RADIX)
    index = k1[:, None, None] * r[None, None, :] + outer * (r[:, None] * r[None, :])[None]
    phase = 2.0 * np.pi * (index % padded) / padded
    cos, sin = np.cos(phase), np.sin(phase)
    table = np.concatenate(
        [np.concatenate([cos, sin], axis=2), np.concatenate([-sin, cos], axis=2)], axis=1
    )
    there = jnp.asarray(table.astype(ml_dtypes.bfloat16))
    back = jnp.asarray(np.swapaxes(table, 1, 2).astype(ml_dtypes.bfloat16))
    return there, back


def real_forward(points):
    size = len(points)
    if size == 2:
        if points[1] is None:
            return [points[0], points[0]], [None, None]
        return [points[0] + points[1], points[0] - points[1]], [None, None]
    even_re, even_im = real_forward(points[0::2])
    odd_re, odd_im = real_forward(points[1::2])
    half = size // 2
    re, im = [None] * (half + 1), [None] * (half + 1)
    re[0], re[half] = even_re[0] + odd_re[0], even_re[0] - odd_re[0]
    for k in range(1, half // 2):
        cos = math.cos(2.0 * math.pi * k / size)
        sin = math.sin(2.0 * math.pi * k / size)
        turn_re = cos * odd_re[k] + sin * odd_im[k]
        turn_im = cos * odd_im[k] - sin * odd_re[k]
        re[k], im[k] = even_re[k] + turn_re, even_im[k] + turn_im
        re[half - k], im[half - k] = even_re[k] - turn_re, turn_im - even_im[k]
    re[half // 2], im[half // 2] = even_re[half // 2], -odd_re[half // 2]
    return re, im


def real_backward(re, im, wanted):
    half = len(re) - 1
    size = 2 * half
    if size == 2:
        return [re[0] + re[1]] + ([re[0] - re[1]] if wanted > 1 else [None])
    quarter = half // 2
    even_re, even_im = [None] * (quarter + 1), [None] * (quarter + 1)
    odd_re, odd_im = [None] * (quarter + 1), [None] * (quarter + 1)
    even_re[0], odd_re[0] = re[0] + re[half], re[0] - re[half]
    for k in range(1, quarter):
        cos = math.cos(2.0 * math.pi * k / size)
        sin = math.sin(2.0 * math.pi * k / size)
        even_re[k], even_im[k] = re[k] + re[half - k], im[k] - im[half - k]
        diff_re, diff_im = re[k] - re[half - k], im[k] + im[half - k]
        odd_re[k] = cos * diff_re - sin * diff_im
        odd_im[k] = cos * diff_im + sin * diff_re
    even_re[quarter], odd_re[quarter] = 2.0 * re[quarter], -2.0 * im[quarter]
    even = real_backward(even_re, even_im, wanted // 2)
    odd = real_backward(odd_re, odd_im, wanted // 2)
    return [point for pair in zip(even, odd) for point in pair]


def load_points(ref, chunk, half):
    per = ref.shape[1] // RADIX
    return [ref[p // per, pl.ds((p % per) * RADIX + chunk * STEP, STEP), :] for p in range(half)]


def outer_forward(x_ref, mid_ref):
    half = mid_ref.shape[0] - 1

    def chunk_body(chunk, carry):
        points = [x.astype(F32) for x in load_points(x_ref, chunk, half)]
        re, im = real_forward(points + [None] * half)
        for k in range(half + 1):
            mid_ref[k, pl.ds(chunk * STEP, STEP), :] = re[k].astype(BF16)
            low = jnp.zeros_like(re[k]) if im[k] is None else im[k]
            mid_ref[k, pl.ds(RADIX + chunk * STEP, STEP), :] = low.astype(BF16)
        return carry

    lax.fori_loop(0, RADIX // STEP, chunk_body, 0)


def outer_backward(mid_ref, chunk, scale):
    half = mid_ref.shape[0] - 1
    re = [mid_ref[k, pl.ds(chunk * STEP, STEP), :].astype(F32) for k in range(half + 1)]
    im = [
        mid_ref[k, pl.ds(RADIX + chunk * STEP, STEP), :].astype(F32) if 0 < k < half else None
        for k in range(half + 1)
    ]
    return [scale * point for point in real_backward(re, im, half)[:half]]


def matmul(a, b):
    return jnp.dot(a, b, preferred_element_type=F32)


def product(a, b):
    a_re, a_im, b_re, b_im = a[:RADIX], a[RADIX:], b[:RADIX], b[RADIX:]
    return jnp.concatenate([a_re * b_re - a_im * b_im, a_re * b_im + a_im * b_re]).astype(BF16)


def conj_product(a, b):
    a_re, a_im, b_re, b_im = a[:RADIX], a[RADIX:], b[:RADIX], b[RADIX:]
    return jnp.concatenate([a_re * b_re + a_im * b_im, a_re * b_im - a_im * b_re]).astype(BF16)


def conv_kernel(v_ref, k_ref, there_ref, back_ref, spec_v_ref, spec_k_ref, out_ref, mid_v, mid_k):
    half = mid_v.shape[0] - 1
    scale = 0.5 / (half * RADIX)
    outer_forward(v_ref, mid_v)
    outer_forward(k_ref, mid_k)

    def freq_body(k, carry):
        spec_v = matmul(there_ref[k], mid_v[k])
        spec_k = matmul(there_ref[k], mid_k[k])
        spec_v_ref[k] = spec_v
        spec_k_ref[k] = spec_k
        mid_v[k] = matmul(back_ref[k], product(spec_v, spec_k)).astype(BF16)
        return carry

    lax.fori_loop(0, half + 1, freq_body, 0)
    per = out_ref.shape[1] // RADIX

    def chunk_body(chunk, carry):
        for p, point in enumerate(outer_backward(mid_v, chunk, scale)):
            rows = pl.ds((p % per) * RADIX + chunk * STEP, STEP)
            out_ref[p // per, rows, :] = point.astype(BF16)
        return carry

    lax.fori_loop(0, RADIX // STEP, chunk_body, 0)


def grad_kernel(
    g_ref, k_ref, spec_v_ref, spec_k_ref, there_ref, back_ref, cg_ref, kg_ref, mid_g, mid_c
):
    half = mid_g.shape[0] - 1
    length = half * RADIX
    scale = 0.5 / length
    outer_forward(g_ref, mid_g)

    def freq_body(k, carry):
        spec_g = matmul(there_ref[k], mid_g[k])
        back = back_ref[k]
        mid_c[k] = matmul(back, conj_product(spec_k_ref[k], spec_g)).astype(BF16)
        mid_g[k] = matmul(back, conj_product(spec_v_ref[k], spec_g)).astype(BF16)
        return carry

    lax.fori_loop(0, half + 1, freq_body, 0)
    rows = g_ref.shape[1]
    per = rows // RADIX

    def chunk_body(chunk, total):
        for p, point in enumerate(outer_backward(mid_c, chunk, scale)):
            here = pl.ds((p % per) * RADIX + chunk * STEP, STEP)
            cg_ref[p // per, here, :] = point.astype(BF16)
        kernel = load_points(k_ref, chunk, half)
        first = lax.broadcasted_iota(jnp.int32, total.shape, 0) + chunk * STEP
        for p, point in enumerate(outer_backward(mid_g, chunk, scale)):
            here = pl.ds((p % per) * RADIX + chunk * STEP, STEP)
            kg_ref[p // per, here, :] = point.astype(BF16)
            place = (first + p * RADIX).astype(F32) * (1.0 / length)
            total = total + place * point * kernel[p].astype(F32)
        return total

    total = jnp.zeros((STEP, g_ref.shape[2]), F32)
    total = lax.fori_loop(0, RADIX // STEP, chunk_body, total)
    total = -(1.0 / math.sqrt(length)) * jnp.sum(total, axis=0, keepdims=True)
    high = total.astype(BF16).astype(F32)
    row = lax.broadcasted_iota(jnp.int32, (STEP, g_ref.shape[2]), 0)
    extra = jnp.where(row == 0, high, jnp.where(row == 1, total - high, 0.0)).astype(BF16)
    for device in range(kg_ref.shape[0]):
        kg_ref[device, pl.ds(rows, STEP), :] = extra


def pack_kernel(v_ref, filt_ref, decay_ref, start_ref, out_ref, *, length):
    own = out_ref.shape[3]
    rows = v_ref.shape[0]
    row = lax.broadcasted_iota(jnp.int32, (rows, own), 0) + start_ref[0]
    position = row.astype(F32) * (1.0 / length)
    for d in range(out_ref.shape[0]):
        cols = slice(d * own, (d + 1) * own)
        out_ref[d, 0] = v_ref[:, cols]
        window = jnp.exp(-decay_ref[:, cols] * position)
        out_ref[d, 1] = (filt_ref[:, cols] * window * (1.0 / math.sqrt(length))).astype(BF16)


def gated_kernel(grad_ref, gate_ref, out_ref):
    own = out_ref.shape[2]
    for d in range(out_ref.shape[0]):
        cols = slice(d * own, (d + 1) * own)
        out_ref[d] = (grad_ref[:, cols].astype(F32) * gate_ref[:, cols].astype(F32)).astype(BF16)


def out_kernel(moved_ref, grad_ref, gate_ref, d_gate_ref, gated_ref):
    own = moved_ref.shape[2]
    for d in range(moved_ref.shape[0]):
        cols = slice(d * own, (d + 1) * own)
        conv_out = moved_ref[d].astype(F32)
        d_gate_ref[:, cols] = (grad_ref[:, cols].astype(F32) * conv_out).astype(BF16)
        gated_ref[:, cols] = (gate_ref[:, cols].astype(F32) * conv_out).astype(BF16)


def values_kernel(moved_ref, out_ref):
    own = moved_ref.shape[2]
    for d in range(moved_ref.shape[0]):
        out_ref[:, slice(d * own, (d + 1) * own)] = moved_ref[d]


def filt_kernel(moved_ref, decay_ref, start_ref, d_filt_ref, decay_grad_ref, *, length):
    own = moved_ref.shape[2]
    rows = d_filt_ref.shape[0]
    row = lax.broadcasted_iota(jnp.int32, (rows, own), 0) + start_ref[0]
    position = row.astype(F32) * (1.0 / length)
    for d in range(moved_ref.shape[0]):
        cols = slice(d * own, (d + 1) * own)
        window = jnp.exp(-decay_ref[:, cols] * position)
        kernel_grad = moved_ref[d, pl.ds(0, rows), :].astype(F32)
        d_filt_ref[:, cols] = kernel_grad * window * (1.0 / math.sqrt(length))
        extra = moved_ref[d, pl.ds(rows, STEP), :].astype(F32)
        decay_grad_ref[:, cols] = extra[0:1] + extra[1:2]


def call(kernel, outs, args, scratch=(), flops=0, scalar=()):
    whole = pl.BlockSpec(memory_space=pltpu.VMEM)
    specs = [
        pl.BlockSpec(memory_space=pltpu.SMEM) if i in scalar else whole for i in range(len(args))
    ]
    moved = sum(math.prod(a.shape) * a.dtype.itemsize for a in (*args, *outs))
    return pl.pallas_call(
        kernel,
        out_shape=outs,
        in_specs=specs,
        out_specs=[whole] * len(outs),
        scratch_shapes=list(scratch),
        compiler_params=pltpu.CompilerParams(vmem_limit_bytes=VMEM_BYTES),
        cost_estimate=pl.CostEstimate(flops=flops, bytes_accessed=moved, transcendentals=0),
    )(*args)


def struct(shape, dtype):
    return jax.ShapeDtypeStruct(shape, dtype)


def swap(array, axis, size, bit):
    return lax.ppermute(array, axis, [(i, i ^ bit) for i in range(size)])


def gather_columns(block, axis):
    size = lax.axis_size(axis)
    if size != 2:
        return lax.all_gather(block, axis, axis=1, tiled=True)
    other = swap(block, axis, size, 1)
    first = lax.axis_index(axis) == 0
    return jnp.concatenate(
        [jnp.where(first, block, other), jnp.where(first, other, block)], axis=1
    )


def line_reduce_scatter(parts, size, inner, beside):
    outer = size // inner
    z = lax.axis_index("seq") // inner
    total = lax.dynamic_index_in_dim(parts, z, 0, keepdims=False).astype(F32)
    right = left = None
    for step in range(1, outer):
        ahead = lax.dynamic_index_in_dim(
            parts, jnp.minimum(z + outer - step, outer - 1), 0, keepdims=False
        )
        behind = lax.dynamic_index_in_dim(
            parts, jnp.maximum(z - outer + step, 0), 0, keepdims=False
        )
        if right is not None:
            ahead = (ahead.astype(F32) + right.astype(F32)).astype(BF16)
            behind = (behind.astype(F32) + left.astype(F32)).astype(BF16)
        to_right = [(i, i + inner) for i in range(size) if i // inner < step]
        to_left = [(i, i - inner) for i in range(size) if i // inner >= outer - step]
        right = lax.ppermute(ahead, "seq", to_right)
        left = lax.ppermute(behind, "seq", to_left)
        if step == 1:
            right, left, beside = lax.optimization_barrier((right, left, beside))
    if right is not None:
        total = total + right.astype(F32) + left.astype(F32)
    return total, beside


def exchange(blocks):
    return lax.all_to_all(blocks, "seq", split_axis=0, concat_axis=0, tiled=True)


def on_device(values, gate, out_grad, out_weight, filt, decay):
    rows, width = values.shape
    seq = lax.axis_size("seq")
    me = lax.axis_index("seq")
    length = rows * seq
    own = width // seq
    norm_scale = 1.0 / math.sqrt(length)
    inner = 4 if seq % 4 == 0 else 1
    outer = seq // inner
    half = length // RADIX
    there, back = middle_tables(length)
    blocks = struct((seq, rows, own), BF16)
    spectrum = struct((half + 1, 2 * RADIX, own), F32)
    mid = pltpu.VMEM((half + 1, 2 * RADIX, own), BF16)
    inner_flops = 2 * (half + 1) * (2 * RADIX) ** 2 * own
    start = (me * rows).astype(jnp.int32)[None]
    rates = decay[None, :]

    full_grad = gather_columns(out_grad, "tp")
    (packed,) = call(
        functools.partial(pack_kernel, length=length),
        [struct((seq, 2, rows, own), BF16)],
        (values, filt, rates, start),
        scalar=(3,),
    )
    moved = exchange(packed)

    grad_y = jnp.dot(full_grad, out_weight, preferred_element_type=F32).astype(BF16)
    (gated_grad,) = call(gated_kernel, [blocks], (grad_y, gate))
    gated_grad, moved = lax.optimization_barrier((gated_grad, moved))
    grad_c = exchange(gated_grad)

    features = full_grad.shape[1] // seq
    by_inner = full_grad.reshape(rows, outer, inner, features)
    bits = [0]
    high = inner // 2
    while high:
        bits = bits + [bit ^ high for bit in bits]
        high //= 2
    grads = []
    for bit in bits:
        target = (me % inner) ^ bit
        piece = lax.dynamic_index_in_dim(by_inner, target, 2, keepdims=False)
        piece = piece.reshape(rows, outer * features)
        grads.append(swap(piece, "seq", seq, bit) if bit else piece)
    grads = jnp.concatenate(grads, axis=0)

    values_c, kernel_c = moved[:, 0], moved[:, 1]
    spec_v, spec_k, conv_out_c = call(
        conv_kernel,
        [spectrum, spectrum, blocks],
        (values_c, kernel_c, there, back),
        scratch=(mid, mid),
        flops=6 * inner_flops,
    )
    conv_out_c, grad_c, grads = lax.optimization_barrier((conv_out_c, grad_c, grads))
    conv_out = exchange(conv_out_c)

    conv_grad_c, kernel_grad_c = call(
        grad_kernel,
        [blocks, struct((seq, rows + STEP, own), BF16)],
        (grad_c, kernel_c, spec_v, spec_k, there, back),
        scratch=(mid, mid),
        flops=6 * inner_flops,
    )
    conv_grad_c, kernel_grad_c, conv_out = lax.optimization_barrier(
        (conv_grad_c, kernel_grad_c, conv_out)
    )
    conv_grad = exchange(conv_grad_c)

    block = struct((rows, width), BF16)
    d_gate, gated_out = call(out_kernel, [block, block], (conv_out, grad_y, gate))
    outs = [gated_out]
    high = inner // 2
    while high:
        outs = outs + [swap(part, "seq", seq, high) for part in outs]
        high //= 2
    *outs, conv_grad, kernel_grad_c = lax.optimization_barrier(
        (*outs, conv_grad, kernel_grad_c)
    )
    kernel_grad = exchange(kernel_grad_c)
    (d_values,) = call(values_kernel, [block], (conv_grad,))
    terms = lax.dot_general(
        grads,
        jnp.concatenate(outs, axis=0),
        (((0,), (0,)), ((), ())),
        preferred_element_type=F32,
    ).astype(BF16)
    terms = terms.reshape(outer, features, width)
    total, kernel_grad = line_reduce_scatter(terms, seq, inner, kernel_grad)
    d_out_weight = total * norm_scale
    d_filt, decay_grad = call(
        functools.partial(filt_kernel, length=length),
        [struct((rows, width), F32), struct((1, width), F32)],
        (kernel_grad, rates, start),
        scalar=(2,),
    )
    return (d_values, d_gate, d_filt, decay_grad[0], d_out_weight)


def solution(mesh):
    in_specs = (
        P("seq", "tp"),
        P("seq", "tp"),
        P("seq", "tp"),
        P(None, "tp"),
        P("seq", "tp"),
        P("tp"),
    )
    out_specs = (P("seq", "tp"), P("seq", "tp"), P("seq", "tp"), P("tp"), P("seq", "tp"))
    return jax.shard_map(
        on_device, mesh=mesh, in_specs=in_specs, out_specs=out_specs, check_vma=False
    )
```

```python
import functools
import math

import jax
import jax.numpy as jnp
import ml_dtypes
import numpy as np
from jax import lax
from jax.experimental import pallas as pl
from jax.experimental.pallas import tpu as pltpu
from jax.sharding import PartitionSpec as P

BF16 = jnp.bfloat16
F32 = jnp.float32
RADIX = 128
STEP = 16
VMEM_BYTES = 48 * 1024 * 1024


def middle_tables(length):
    padded = 2 * length
    outer = padded // RADIX
    k1 = np.arange(outer // 2 + 1)
    r = np.arange(RADIX)
    index = k1[:, None, None] * r[None, None, :] + outer * (r[:, None] * r[None, :])[None]
    phase = 2.0 * np.pi * (index % padded) / padded
    cos, sin = np.cos(phase), np.sin(phase)
    table = np.concatenate(
        [np.concatenate([cos, sin], axis=2), np.concatenate([-sin, cos], axis=2)], axis=1
    )
    there = jnp.asarray(table.astype(ml_dtypes.bfloat16))
    back = jnp.asarray(np.swapaxes(table, 1, 2).astype(ml_dtypes.bfloat16))
    return there, back


def real_forward(points):
    size = len(points)
    if size == 2:
        if points[1] is None:
            return [points[0], points[0]], [None, None]
        return [points[0] + points[1], points[0] - points[1]], [None, None]
    even_re, even_im = real_forward(points[0::2])
    odd_re, odd_im = real_forward(points[1::2])
    half = size // 2
    re, im = [None] * (half + 1), [None] * (half + 1)
    re[0], re[half] = even_re[0] + odd_re[0], even_re[0] - odd_re[0]
    for k in range(1, half // 2):
        cos = math.cos(2.0 * math.pi * k / size)
        sin = math.sin(2.0 * math.pi * k / size)
        turn_re = cos * odd_re[k] + sin * odd_im[k]
        turn_im = cos * odd_im[k] - sin * odd_re[k]
        re[k], im[k] = even_re[k] + turn_re, even_im[k] + turn_im
        re[half - k], im[half - k] = even_re[k] - turn_re, turn_im - even_im[k]
    re[half // 2], im[half // 2] = even_re[half // 2], -odd_re[half // 2]
    return re, im


def real_backward(re, im, wanted):
    half = len(re) - 1
    size = 2 * half
    if size == 2:
        return [re[0] + re[1]] + ([re[0] - re[1]] if wanted > 1 else [None])
    quarter = half // 2
    even_re, even_im = [None] * (quarter + 1), [None] * (quarter + 1)
    odd_re, odd_im = [None] * (quarter + 1), [None] * (quarter + 1)
    even_re[0], odd_re[0] = re[0] + re[half], re[0] - re[half]
    for k in range(1, quarter):
        cos = math.cos(2.0 * math.pi * k / size)
        sin = math.sin(2.0 * math.pi * k / size)
        even_re[k], even_im[k] = re[k] + re[half - k], im[k] - im[half - k]
        diff_re, diff_im = re[k] - re[half - k], im[k] + im[half - k]
        odd_re[k] = cos * diff_re - sin * diff_im
        odd_im[k] = cos * diff_im + sin * diff_re
    even_re[quarter], odd_re[quarter] = 2.0 * re[quarter], -2.0 * im[quarter]
    even = real_backward(even_re, even_im, wanted // 2)
    odd = real_backward(odd_re, odd_im, wanted // 2)
    return [point for pair in zip(even, odd) for point in pair]


def load_points(ref, chunk, half):
    per = ref.shape[1] // RADIX
    return [ref[p // per, pl.ds((p % per) * RADIX + chunk * STEP, STEP), :] for p in range(half)]


def outer_forward(x_ref, mid_ref, lanes):
    half = mid_ref.shape[0] - 1

    def chunk_body(chunk, carry):
        points = [x.astype(F32) for x in load_points(x_ref, chunk, half)]
        re, im = real_forward(points + [None] * half)
        for k in range(half + 1):
            mid_ref[k, pl.ds(chunk * STEP, STEP), lanes] = re[k].astype(BF16)
            low = jnp.zeros_like(re[k]) if im[k] is None else im[k]
            mid_ref[k, pl.ds(RADIX + chunk * STEP, STEP), lanes] = low.astype(BF16)
        return carry

    lax.fori_loop(0, RADIX // STEP, chunk_body, 0)


def outer_backward(mid_ref, chunk, scale, lanes):
    half = mid_ref.shape[0] - 1
    re = [mid_ref[k, pl.ds(chunk * STEP, STEP), lanes].astype(F32) for k in range(half + 1)]
    im = [
        mid_ref[k, pl.ds(RADIX + chunk * STEP, STEP), lanes].astype(F32) if 0 < k < half else None
        for k in range(half + 1)
    ]
    return [scale * point for point in real_backward(re, im, half)[:half]]


def matmul(a, b):
    return jnp.dot(a, b, preferred_element_type=F32)


def product(a, b):
    a_re, a_im, b_re, b_im = a[:RADIX], a[RADIX:], b[:RADIX], b[RADIX:]
    return jnp.concatenate([a_re * b_re - a_im * b_im, a_re * b_im + a_im * b_re]).astype(BF16)


def conj_product(a, b):
    a_re, a_im, b_re, b_im = a[:RADIX], a[RADIX:], b[:RADIX], b[RADIX:]
    return jnp.concatenate([a_re * b_re + a_im * b_im, a_re * b_im - a_im * b_re]).astype(BF16)


def unrolled(count):
    return max(d for d in range(1, 14) if count % d == 0)


def conv_kernel(v_ref, k_ref, there_ref, back_ref, spec_ref, out_ref, mid):
    half = mid.shape[0] - 1
    own = out_ref.shape[2]
    low, high = slice(0, own), slice(own, 2 * own)
    scale = 0.5 / (half * RADIX)
    outer_forward(v_ref, mid, low)
    outer_forward(k_ref, mid, high)

    def freq_body(k, carry):
        spec = matmul(there_ref[k], mid[k])
        spec_ref[k] = spec
        mid[k, :, low] = matmul(back_ref[k], product(spec[:, low], spec[:, high])).astype(BF16)
        return carry

    lax.fori_loop(0, half + 1, freq_body, 0, unroll=unrolled(half + 1))
    per = out_ref.shape[1] // RADIX

    def chunk_body(chunk, carry):
        for p, point in enumerate(outer_backward(mid, chunk, scale, low)):
            rows = pl.ds((p % per) * RADIX + chunk * STEP, STEP)
            out_ref[p // per, rows, :] = point.astype(BF16)
        return carry

    lax.fori_loop(0, RADIX // STEP, chunk_body, 0)


def grad_kernel(g_ref, k_ref, spec_ref, there_ref, back_ref, cg_ref, kg_ref, mid):
    half = mid.shape[0] - 1
    length = half * RADIX
    own = cg_ref.shape[2]
    low, high = slice(0, own), slice(own, 2 * own)
    scale = 0.5 / length
    outer_forward(g_ref, mid, low)

    def freq_body(k, carry):
        spec_g = matmul(there_ref[k], mid[k, :, low])
        both = jnp.concatenate([spec_g, spec_g], axis=1)
        mid[k] = matmul(back_ref[k], conj_product(spec_ref[k], both)).astype(BF16)
        return carry

    lax.fori_loop(0, half + 1, freq_body, 0, unroll=unrolled(half + 1))
    rows = g_ref.shape[1]
    per = rows // RADIX

    def chunk_body(chunk, total):
        for p, point in enumerate(outer_backward(mid, chunk, scale, high)):
            here = pl.ds((p % per) * RADIX + chunk * STEP, STEP)
            cg_ref[p // per, here, :] = point.astype(BF16)
        kernel = load_points(k_ref, chunk, half)
        first = lax.broadcasted_iota(jnp.int32, total.shape, 0) + chunk * STEP
        for p, point in enumerate(outer_backward(mid, chunk, scale, low)):
            here = pl.ds((p % per) * RADIX + chunk * STEP, STEP)
            kg_ref[p // per, here, :] = point.astype(BF16)
            place = (first + p * RADIX).astype(F32) * (1.0 / length)
            total = total + place * point * kernel[p].astype(F32)
        return total

    total = jnp.zeros((STEP, g_ref.shape[2]), F32)
    total = lax.fori_loop(0, RADIX // STEP, chunk_body, total)
    total = -(1.0 / math.sqrt(length)) * jnp.sum(total, axis=0, keepdims=True)
    high = total.astype(BF16).astype(F32)
    row = lax.broadcasted_iota(jnp.int32, (STEP, g_ref.shape[2]), 0)
    extra = jnp.where(row == 0, high, jnp.where(row == 1, total - high, 0.0)).astype(BF16)
    for device in range(kg_ref.shape[0]):
        kg_ref[device, pl.ds(rows, STEP), :] = extra


def pack_kernel(v_ref, filt_ref, decay_ref, start_ref, out_ref, *, length):
    own = out_ref.shape[3]
    rows = v_ref.shape[0]
    row = lax.broadcasted_iota(jnp.int32, (rows, own), 0) + start_ref[0]
    position = row.astype(F32) * (1.0 / length)
    for d in range(out_ref.shape[0]):
        cols = slice(d * own, (d + 1) * own)
        out_ref[d, 0] = v_ref[:, cols]
        window = jnp.exp(-decay_ref[:, cols] * position)
        out_ref[d, 1] = (filt_ref[:, cols] * window * (1.0 / math.sqrt(length))).astype(BF16)


def gated_kernel(grad_ref, gate_ref, out_ref):
    own = out_ref.shape[2]
    for d in range(out_ref.shape[0]):
        cols = slice(d * own, (d + 1) * own)
        out_ref[d] = (grad_ref[:, cols].astype(F32) * gate_ref[:, cols].astype(F32)).astype(BF16)


def layer_pack_kernel(gate_ref, place_ref, out_ref):
    inner, outer, _, own = out_ref.shape
    for z in range(outer):
        for w in range(inner):
            first = (z * inner + w) * own
            out_ref[place_ref[0] ^ w, z] = gate_ref[:, slice(first, first + own)]


def layer_kernel(*refs, order):
    count = len(order)
    gates, gated_refs, homes = refs[:count], refs[count + 2 : -count], refs[-count:]
    moved_ref, place_ref = refs[count : count + 2]
    outer, _, rows, own = moved_ref.shape
    per = outer // len(gated_refs)
    for i, bit in enumerate(order):
        for z in range(outer):
            conv_out = moved_ref[z, place_ref[0] ^ bit]
            homes[i][z] = conv_out
            gated = (gates[i][z].astype(F32) * conv_out.astype(F32)).astype(BF16)
            first = (z % per) * own
            gated_refs[z // per][pl.ds(i * rows, rows), slice(first, first + own)] = gated


def gate_kernel(moved_ref, grad_ref, place_ref, out_ref):
    inner, outer, _, own = moved_ref.shape
    for z in range(outer):
        for w in range(inner):
            cols = slice((z * inner + w) * own, (z * inner + w + 1) * own)
            conv_out = moved_ref[place_ref[0] ^ w, z].astype(F32)
            out_ref[:, cols] = (grad_ref[:, cols].astype(F32) * conv_out).astype(BF16)


def weight_kernel(moved_ref, place_ref, out_ref, *, scale, own):
    chunks, inner, _, wide = moved_ref.shape
    per = wide // own
    for z in range(chunks * per):
        for w in range(inner):
            cols = slice((z * inner + w) * own, (z * inner + w + 1) * own)
            first = (z % per) * own
            part = moved_ref[z // per, place_ref[0] ^ w, :, slice(first, first + own)]
            out_ref[:, cols] = part.astype(F32) * scale


def transpose_kernel(x_ref, out_ref):
    rows = x_ref.shape[0]
    for first in range(0, x_ref.shape[1], rows):
        out_ref[pl.ds(first, rows), :] = x_ref[:, slice(first, first + rows)].T


def values_kernel(moved_ref, out_ref):
    own = moved_ref.shape[2]
    for d in range(moved_ref.shape[0]):
        out_ref[:, slice(d * own, (d + 1) * own)] = moved_ref[d]


def filt_kernel(moved_ref, decay_ref, start_ref, d_filt_ref, decay_grad_ref, *, length):
    own = moved_ref.shape[2]
    rows = d_filt_ref.shape[0]
    row = lax.broadcasted_iota(jnp.int32, (rows, own), 0) + start_ref[0]
    position = row.astype(F32) * (1.0 / length)
    for d in range(moved_ref.shape[0]):
        cols = slice(d * own, (d + 1) * own)
        window = jnp.exp(-decay_ref[:, cols] * position)
        kernel_grad = moved_ref[d, pl.ds(0, rows), :].astype(F32)
        d_filt_ref[:, cols] = kernel_grad * window * (1.0 / math.sqrt(length))
        extra = moved_ref[d, pl.ds(rows, STEP), :].astype(F32)
        decay_grad_ref[:, cols] = extra[0:1] + extra[1:2]


def call(kernel, outs, args, scratch=(), flops=0, scalar=()):
    whole = pl.BlockSpec(memory_space=pltpu.VMEM)
    specs = [
        pl.BlockSpec(memory_space=pltpu.SMEM) if i in scalar else whole for i in range(len(args))
    ]
    moved = sum(math.prod(a.shape) * a.dtype.itemsize for a in (*args, *outs))
    return pl.pallas_call(
        kernel,
        out_shape=outs,
        in_specs=specs,
        out_specs=[whole] * len(outs),
        scratch_shapes=list(scratch),
        compiler_params=pltpu.CompilerParams(vmem_limit_bytes=VMEM_BYTES),
        cost_estimate=pl.CostEstimate(flops=flops, bytes_accessed=moved, transcendentals=0),
    )(*args)


def struct(shape, dtype):
    return jax.ShapeDtypeStruct(shape, dtype)


def swap(array, axis, size, bit):
    return lax.ppermute(array, axis, [(i, i ^ bit) for i in range(size)])


def gather_columns(block, axis):
    size = lax.axis_size(axis)
    if size != 2:
        whole = lax.all_gather(block, axis, axis=1, tiled=True)
        return [whole], whole
    other = swap(block, axis, size, 1)
    first = lax.axis_index(axis) == 0
    return [block, other], jnp.concatenate(
        [jnp.where(first, block, other), jnp.where(first, other, block)], axis=1
    )


def turn(part):
    return call(transpose_kernel, [struct(part.shape[::-1], BF16)], (part,))[0]


def layer_grads(halves, inner, after):
    order = [0]
    bit = inner // 2
    while bit:
        order = order + [i ^ bit for i in order]
        bit //= 2
    turned = [turn(part) for part in halves]
    if inner == 1:
        return order, [[part] for part in turned]
    seq = lax.axis_size("seq")
    across = [swap(turned[0], "seq", seq, inner // 2)]
    if len(turned) == 2:
        late, _ = lax.optimization_barrier((across[0], after))
        across.append(swap(late, "tp", 2, 1))
    return order, [list(pair) for pair in zip(turned, across)]


def outer_kernel(*refs, groups, tiles):
    *lhs_refs, rhs_ref, out_ref = refs
    count = len(lhs_refs) // groups
    depth = lhs_refs[0].shape[1]
    for group in range(groups):

        @pl.when(pl.program_id(0) // tiles == group)
        def _():
            total = 0.0
            for i, ref in enumerate(lhs_refs[group * count : (group + 1) * count]):
                total = total + matmul(ref[...], rhs_ref[pl.ds(i * depth, depth), :])
            out_ref[...] = total.astype(BF16)


def outer_product(groups, rhs):
    rows, depth = groups[0][0].shape
    tile = math.gcd(rows, 1024)
    tiles = rows // tile
    wide = rhs.shape[1]

    def lhs_spec(group):
        return pl.BlockSpec(
            (tile, depth), lambda i: (jnp.clip(i - group * tiles, 0, tiles - 1), 0)
        )

    flat = [part for group in groups for part in group]
    total = rows * len(groups)
    return pl.pallas_call(
        functools.partial(outer_kernel, groups=len(groups), tiles=tiles),
        grid=(len(groups) * tiles,),
        out_shape=struct((total, wide), BF16),
        in_specs=[lhs_spec(i) for i, group in enumerate(groups) for _ in group]
        + [pl.BlockSpec(rhs.shape, lambda i: (0, 0))],
        out_specs=pl.BlockSpec((tile, wide), lambda i: (i, 0)),
        compiler_params=pltpu.CompilerParams(vmem_limit_bytes=VMEM_BYTES),
        cost_estimate=pl.CostEstimate(
            flops=4 * total * rhs.shape[0] * wide,
            bytes_accessed=2 * (len(flat) * rows * depth + total * wide),
            transcendentals=0,
        ),
    )(*flat, rhs)


def line_reduce_scatter(chunks, size, inner, shift, beside, later):
    outer = size // inner
    z = lax.axis_index("seq") // inner

    def block_of(parts, at):
        return lax.dynamic_index_in_dim(parts, at ^ shift, 0, keepdims=False)

    totals = [block_of(parts, z).astype(F32) for parts in chunks]
    flows = [None] * len(chunks)
    for step in range(1, outer):
        to_right = [(i, i + inner) for i in range(size) if i // inner < step]
        to_left = [(i, i - inner) for i in range(size) if i // inner >= outer - step]
        for i, parts in enumerate(chunks):
            ahead = block_of(parts, jnp.minimum(z + outer - step, outer - 1))
            behind = block_of(parts, jnp.maximum(z - outer + step, 0))
            if flows[i] is not None:
                right, left = lax.optimization_barrier(flows[i])
                ahead = (ahead.astype(F32) + right.astype(F32)).astype(BF16)
                behind = (behind.astype(F32) + left.astype(F32)).astype(BF16)
                ahead, behind = lax.optimization_barrier((ahead, behind))
            flows[i] = (
                lax.ppermute(ahead, "seq", to_right),
                lax.ppermute(behind, "seq", to_left),
            )
        if step == 1:
            *flows[-1], beside, later = lax.optimization_barrier((*flows[-1], beside, later))
    if outer > 1:
        totals = [
            total + right.astype(F32) + left.astype(F32)
            for total, (right, left) in zip(totals, flows)
        ]
    return totals, beside, later


def exchange(blocks, groups=None):
    return lax.all_to_all(
        blocks, "seq", split_axis=0, concat_axis=0, tiled=True, axis_index_groups=groups
    )


def on_device(values, gate, out_grad, out_weight, filt, decay):
    rows, width = values.shape
    seq = lax.axis_size("seq")
    me = lax.axis_index("seq")
    length = rows * seq
    own = width // seq
    norm_scale = 1.0 / math.sqrt(length)
    inner = 4 if seq % 4 == 0 else 1
    outer = seq // inner
    half = length // RADIX
    there, back = middle_tables(length)
    blocks = struct((seq, rows, own), BF16)
    spectrum = struct((half + 1, 2 * RADIX, 2 * own), F32)
    mid = pltpu.VMEM((half + 1, 2 * RADIX, 2 * own), BF16)
    work = 300 * (half + 1) * RADIX**2 * own
    start = (me * rows).astype(jnp.int32)[None]
    rates = decay[None, :]

    halves, full_grad = gather_columns(out_grad, "tp")
    (packed,) = call(
        functools.partial(pack_kernel, length=length),
        [struct((seq, 2, rows, own), BF16)],
        (values, filt, rates, start),
        scalar=(3,),
    )
    moved = exchange(packed)

    grad_y = jnp.dot(full_grad, out_weight, preferred_element_type=F32).astype(BF16)
    (gated_grad,) = call(gated_kernel, [blocks], (grad_y, gate))
    gated_grad, moved = lax.optimization_barrier((gated_grad, moved))
    grad_c = exchange(gated_grad)

    values_c, kernel_c = moved[:, 0], moved[:, 1]
    spec, conv_out_c = call(
        conv_kernel,
        [spectrum, blocks],
        (values_c, kernel_c, there, back),
        scratch=(mid,),
        flops=work,
    )
    place = (me % inner).astype(jnp.int32)[None]
    (gates,) = call(
        layer_pack_kernel, [struct((inner, outer, rows, own), BF16)], (gate, place), scalar=(1,)
    )
    gates, _ = lax.optimization_barrier((gates, moved))
    order, grads = layer_grads(halves, inner, conv_out_c)
    gates = [swap(gates[bit], "seq", seq, bit) if bit else gates[bit] for bit in order]
    *gates, conv_out_c = lax.optimization_barrier((*gates, conv_out_c))
    conv_out_c, grad_c = lax.optimization_barrier((conv_out_c, grad_c))
    layers = [[z * inner + w for z in range(outer)] for w in range(inner)]
    conv_out = exchange(conv_out_c.reshape(outer, inner, rows, own), layers)

    conv_grad_c, kernel_grad_c = call(
        grad_kernel,
        [blocks, struct((seq, rows + STEP, own), BF16)],
        (grad_c, kernel_c, spec, there, back),
        scratch=(mid,),
        flops=work,
    )
    flat, _ = lax.optimization_barrier((sum(grads, []), conv_grad_c))
    count = len(flat) // len(grads)
    grads = [flat[i : i + count] for i in range(0, len(flat), count)]
    bit = inner // 4
    while bit:
        grads = [g + [swap(part, "seq", seq, bit) for part in g] for g in grads]
        bit //= 2
    conv_grad_c, kernel_grad_c, conv_out = lax.optimization_barrier(
        (conv_grad_c, kernel_grad_c, conv_out)
    )
    conv_grad = exchange(conv_grad_c)

    block = struct((rows, width), BF16)
    home = struct((outer, rows, own), BF16)
    chunks = 2 if outer % 2 == 0 else 1
    wide = outer * own // chunks
    parts = call(
        functools.partial(layer_kernel, order=order),
        [struct((inner * rows, wide), BF16)] * chunks + [home] * inner,
        (*gates, conv_out, place),
        scalar=(inner + 1,),
    )
    homes = parts[chunks:]
    terms = [outer_product(grads, part).reshape(outer, -1, wide) for part in parts[:chunks]]
    shift = 0
    if len(grads) == 2:
        shift = lax.axis_index("tp") * (outer // 2)

    homes = {bit: swap(part, "seq", seq, bit) if bit else part for bit, part in zip(order, homes)}
    homes = jnp.stack([homes[bit] for bit in range(inner)])
    (d_gate,) = call(gate_kernel, [block], (homes, grad_y, place), scalar=(2,))
    totals, conv_grad, kernel_grad_c = line_reduce_scatter(
        terms, seq, inner, shift, conv_grad, kernel_grad_c
    )
    kernel_grad = exchange(kernel_grad_c)
    (d_values,) = call(values_kernel, [block], (conv_grad,))
    pieces = []
    for total in totals:
        total = total.astype(BF16).reshape(inner, -1, wide)
        for bit in range(inner):
            piece = lax.dynamic_index_in_dim(total, (me % inner) ^ bit, 0, keepdims=False)
            pieces.append(swap(piece, "seq", seq, bit) if bit else piece)
    pieces = jnp.stack(pieces).reshape(chunks, inner, -1, wide)
    (d_out_weight,) = call(
        functools.partial(weight_kernel, scale=norm_scale, own=own),
        [struct((pieces.shape[2], width), F32)],
        (pieces, place),
        scalar=(1,),
    )
    d_filt, decay_grad = call(
        functools.partial(filt_kernel, length=length),
        [struct((rows, width), F32), struct((1, width), F32)],
        (kernel_grad, rates, start),
        scalar=(2,),
    )
    return (d_values, d_gate, d_filt, decay_grad[0], d_out_weight)


def solution(mesh):
    in_specs = (
        P("seq", "tp"),
        P("seq", "tp"),
        P("seq", "tp"),
        P(None, "tp"),
        P("seq", "tp"),
        P("tp"),
    )
    out_specs = (P("seq", "tp"), P("seq", "tp"), P("seq", "tp"), P("tp"), P("seq", "tp"))
    return jax.shard_map(
        on_device, mesh=mesh, in_specs=in_specs, out_specs=out_specs, check_vma=False
    )
```

```python
import functools
import math

import jax
import jax.numpy as jnp
import ml_dtypes
import numpy as np
from jax import lax
from jax.experimental import pallas as pl
from jax.experimental.pallas import tpu as pltpu
from jax.sharding import PartitionSpec as P

BF16 = jnp.bfloat16
F32 = jnp.float32
RADIX = 128
STEP = 16
VMEM_BYTES = 48 * 1024 * 1024


def middle_tables(length):
    padded = 2 * length
    outer = padded // RADIX
    k1 = np.arange(outer // 2 + 1)
    r = np.arange(RADIX)
    index = k1[:, None, None] * r[None, None, :] + outer * (r[:, None] * r[None, :])[None]
    phase = 2.0 * np.pi * (index % padded) / padded
    cos, sin = np.cos(phase), np.sin(phase)
    table = np.concatenate(
        [np.concatenate([cos, sin], axis=2), np.concatenate([-sin, cos], axis=2)], axis=1
    )
    there = jnp.asarray(table.astype(ml_dtypes.bfloat16))
    back = jnp.asarray(np.swapaxes(table, 1, 2).astype(ml_dtypes.bfloat16))
    return there, back


def real_forward(points):
    size = len(points)
    if size == 2:
        if points[1] is None:
            return [points[0], points[0]], [None, None]
        return [points[0] + points[1], points[0] - points[1]], [None, None]
    even_re, even_im = real_forward(points[0::2])
    odd_re, odd_im = real_forward(points[1::2])
    half = size // 2
    re, im = [None] * (half + 1), [None] * (half + 1)
    re[0], re[half] = even_re[0] + odd_re[0], even_re[0] - odd_re[0]
    for k in range(1, half // 2):
        cos = math.cos(2.0 * math.pi * k / size)
        sin = math.sin(2.0 * math.pi * k / size)
        turn_re = cos * odd_re[k] + sin * odd_im[k]
        turn_im = cos * odd_im[k] - sin * odd_re[k]
        re[k], im[k] = even_re[k] + turn_re, even_im[k] + turn_im
        re[half - k], im[half - k] = even_re[k] - turn_re, turn_im - even_im[k]
    re[half // 2], im[half // 2] = even_re[half // 2], -odd_re[half // 2]
    return re, im


def real_backward(re, im, wanted):
    half = len(re) - 1
    size = 2 * half
    if size == 2:
        return [re[0] + re[1]] + ([re[0] - re[1]] if wanted > 1 else [None])
    quarter = half // 2
    even_re, even_im = [None] * (quarter + 1), [None] * (quarter + 1)
    odd_re, odd_im = [None] * (quarter + 1), [None] * (quarter + 1)
    even_re[0], odd_re[0] = re[0] + re[half], re[0] - re[half]
    for k in range(1, quarter):
        cos = math.cos(2.0 * math.pi * k / size)
        sin = math.sin(2.0 * math.pi * k / size)
        even_re[k], even_im[k] = re[k] + re[half - k], im[k] - im[half - k]
        diff_re, diff_im = re[k] - re[half - k], im[k] + im[half - k]
        odd_re[k] = cos * diff_re - sin * diff_im
        odd_im[k] = cos * diff_im + sin * diff_re
    even_re[quarter], odd_re[quarter] = 2.0 * re[quarter], -2.0 * im[quarter]
    even = real_backward(even_re, even_im, wanted // 2)
    odd = real_backward(odd_re, odd_im, wanted // 2)
    return [point for pair in zip(even, odd) for point in pair]


def load_points(ref, chunk, half, field=0):
    per = ref.shape[2] // RADIX
    return [
        ref[p // per, field, pl.ds((p % per) * RADIX + chunk * STEP, STEP), :] for p in range(half)
    ]


def outer_forward(x_ref, mid_ref, lanes, field=0):
    half = mid_ref.shape[0] - 1

    def chunk_body(chunk, carry):
        points = [x.astype(F32) for x in load_points(x_ref, chunk, half, field)]
        re, im = real_forward(points + [None] * half)
        for k in range(half + 1):
            mid_ref[k, pl.ds(chunk * STEP, STEP), lanes] = re[k].astype(BF16)
            low = jnp.zeros_like(re[k]) if im[k] is None else im[k]
            mid_ref[k, pl.ds(RADIX + chunk * STEP, STEP), lanes] = low.astype(BF16)
        return carry

    lax.fori_loop(0, RADIX // STEP, chunk_body, 0)


def outer_backward(mid_ref, chunk, scale, lanes):
    half = mid_ref.shape[0] - 1
    re = [mid_ref[k, pl.ds(chunk * STEP, STEP), lanes].astype(F32) for k in range(half + 1)]
    im = [
        mid_ref[k, pl.ds(RADIX + chunk * STEP, STEP), lanes].astype(F32) if 0 < k < half else None
        for k in range(half + 1)
    ]
    return [scale * point for point in real_backward(re, im, half)[:half]]


def matmul(a, b):
    return jnp.dot(a, b, preferred_element_type=F32)


def product(a, b):
    a_re, a_im, b_re, b_im = a[:RADIX], a[RADIX:], b[:RADIX], b[RADIX:]
    return jnp.concatenate([a_re * b_re - a_im * b_im, a_re * b_im + a_im * b_re]).astype(BF16)


def conj_product(a, b):
    a_re, a_im, b_re, b_im = a[:RADIX], a[RADIX:], b[:RADIX], b[RADIX:]
    return jnp.concatenate([a_re * b_re + a_im * b_im, a_re * b_im - a_im * b_re]).astype(BF16)


def unrolled(count):
    return max(d for d in range(1, 14) if count % d == 0)


def conv_kernel(fields_ref, there_ref, back_ref, spec_ref, out_ref, mid):
    half = mid.shape[0] - 1
    own = out_ref.shape[2]
    low, high = slice(0, own), slice(own, 2 * own)
    scale = 0.5 / (half * RADIX)
    outer_forward(fields_ref, mid, low, 0)
    outer_forward(fields_ref, mid, high, 1)

    def freq_body(k, carry):
        spec = matmul(there_ref[k], mid[k])
        spec_ref[k] = spec
        mid[k, :, low] = matmul(back_ref[k], product(spec[:, low], spec[:, high])).astype(BF16)
        return carry

    lax.fori_loop(0, half + 1, freq_body, 0, unroll=unrolled(half + 1))
    per = out_ref.shape[1] // RADIX

    def chunk_body(chunk, carry):
        for p, point in enumerate(outer_backward(mid, chunk, scale, low)):
            rows = pl.ds((p % per) * RADIX + chunk * STEP, STEP)
            out_ref[p // per, rows, :] = point.astype(BF16)
        return carry

    lax.fori_loop(0, RADIX // STEP, chunk_body, 0)


def grad_kernel(g_ref, fields_ref, spec_ref, there_ref, back_ref, cg_ref, kg_ref, mid):
    half = mid.shape[0] - 1
    length = half * RADIX
    own = cg_ref.shape[2]
    low, high = slice(0, own), slice(own, 2 * own)
    scale = 0.5 / length
    outer_forward(g_ref, mid, low)

    def freq_body(k, carry):
        spec_g = matmul(there_ref[k], mid[k, :, low])
        both = jnp.concatenate([spec_g, spec_g], axis=1)
        mid[k] = matmul(back_ref[k], conj_product(spec_ref[k], both)).astype(BF16)
        return carry

    lax.fori_loop(0, half + 1, freq_body, 0, unroll=unrolled(half + 1))
    rows = g_ref.shape[2]
    per = rows // RADIX

    def chunk_body(chunk, total):
        for p, point in enumerate(outer_backward(mid, chunk, scale, high)):
            here = pl.ds((p % per) * RADIX + chunk * STEP, STEP)
            cg_ref[p // per, here, :] = point.astype(BF16)
        kernel = load_points(fields_ref, chunk, half, 1)
        first = lax.broadcasted_iota(jnp.int32, total.shape, 0) + chunk * STEP
        for p, point in enumerate(outer_backward(mid, chunk, scale, low)):
            here = pl.ds((p % per) * RADIX + chunk * STEP, STEP)
            kg_ref[p // per, here, :] = point.astype(BF16)
            place = (first + p * RADIX).astype(F32) * (1.0 / length)
            total = total + place * point * kernel[p].astype(F32)
        return total

    total = jnp.zeros((STEP, own), F32)
    total = lax.fori_loop(0, RADIX // STEP, chunk_body, total)
    total = -(1.0 / math.sqrt(length)) * jnp.sum(total, axis=0, keepdims=True)
    leading = total.astype(BF16).astype(F32)
    row = lax.broadcasted_iota(jnp.int32, (STEP, own), 0)
    extra = jnp.where(row == 0, leading, jnp.where(row == 1, total - leading, 0.0)).astype(BF16)
    for device in range(kg_ref.shape[0]):
        kg_ref[device, pl.ds(rows, STEP), :] = extra


def pack_kernel(v_ref, filt_ref, decay_ref, start_ref, out_ref, *, length):
    own = out_ref.shape[3]
    rows = v_ref.shape[0]
    row = lax.broadcasted_iota(jnp.int32, (rows, own), 0) + start_ref[0]
    position = row.astype(F32) * (1.0 / length)
    for d in range(out_ref.shape[0]):
        cols = slice(d * own, (d + 1) * own)
        out_ref[d, 0] = v_ref[:, cols]
        window = jnp.exp(-decay_ref[:, cols] * position)
        out_ref[d, 1] = (filt_ref[:, cols] * window * (1.0 / math.sqrt(length))).astype(BF16)


def gated_kernel(grad_ref, gate_ref, out_ref):
    own = out_ref.shape[3]
    for d in range(out_ref.shape[0]):
        cols = slice(d * own, (d + 1) * own)
        out_ref[d, 0] = (grad_ref[:, cols].astype(F32) * gate_ref[:, cols].astype(F32)).astype(BF16)


def layer_pack_kernel(gate_ref, place_ref, out_ref):
    inner, outer, _, own = out_ref.shape
    for z in range(outer):
        for w in range(inner):
            first = (z * inner + w) * own
            out_ref[place_ref[0] ^ w, z] = gate_ref[:, slice(first, first + own)]


def layer_kernel(*refs, order):
    count = len(order)
    gates, homes = refs[:count], refs[count + 3 :]
    moved_ref, place_ref, gated_ref = refs[count : count + 3]
    outer, _, rows, own = moved_ref.shape
    for i, bit in enumerate(order):
        for z in range(outer):
            conv_out = moved_ref[z, place_ref[0] ^ bit]
            homes[i][z] = conv_out
            gated = (gates[i][z].astype(F32) * conv_out.astype(F32)).astype(BF16)
            gated_ref[pl.ds(i * rows, rows), slice(z * own, (z + 1) * own)] = gated


def gate_kernel(moved_ref, grad_ref, place_ref, out_ref):
    inner, outer, _, own = moved_ref.shape
    for z in range(outer):
        for w in range(inner):
            cols = slice((z * inner + w) * own, (z * inner + w + 1) * own)
            conv_out = moved_ref[place_ref[0] ^ w, z].astype(F32)
            out_ref[:, cols] = (grad_ref[:, cols].astype(F32) * conv_out).astype(BF16)


def weight_kernel(moved_ref, place_ref, out_ref, *, scale, own):
    chunks, inner, _, wide = moved_ref.shape
    per = wide // own
    for z in range(chunks * per):
        for w in range(inner):
            cols = slice((z * inner + w) * own, (z * inner + w + 1) * own)
            first = (z % per) * own
            part = moved_ref[z // per, place_ref[0] ^ w, :, slice(first, first + own)]
            out_ref[:, cols] = part.astype(F32) * scale


def transpose_kernel(x_ref, out_ref):
    rows = x_ref.shape[0]
    for first in range(0, x_ref.shape[1], rows):
        out_ref[pl.ds(first, rows), :] = x_ref[:, slice(first, first + rows)].T


def values_kernel(moved_ref, out_ref):
    own = moved_ref.shape[2]
    for d in range(moved_ref.shape[0]):
        out_ref[:, slice(d * own, (d + 1) * own)] = moved_ref[d]


def filt_kernel(moved_ref, decay_ref, start_ref, d_filt_ref, decay_grad_ref, *, length):
    own = moved_ref.shape[2]
    rows = d_filt_ref.shape[0]
    row = lax.broadcasted_iota(jnp.int32, (rows, own), 0) + start_ref[0]
    position = row.astype(F32) * (1.0 / length)
    for d in range(moved_ref.shape[0]):
        cols = slice(d * own, (d + 1) * own)
        window = jnp.exp(-decay_ref[:, cols] * position)
        kernel_grad = moved_ref[d, pl.ds(0, rows), :].astype(F32)
        d_filt_ref[:, cols] = kernel_grad * window * (1.0 / math.sqrt(length))
        extra = moved_ref[d, pl.ds(rows, STEP), :].astype(F32)
        decay_grad_ref[:, cols] = extra[0:1] + extra[1:2]


def call(kernel, outs, args, scratch=(), flops=0, scalar=()):
    whole = pl.BlockSpec(memory_space=pltpu.VMEM)
    specs = [
        pl.BlockSpec(memory_space=pltpu.SMEM) if i in scalar else whole for i in range(len(args))
    ]
    moved = sum(math.prod(a.shape) * a.dtype.itemsize for a in (*args, *outs))
    return pl.pallas_call(
        kernel,
        out_shape=outs,
        in_specs=specs,
        out_specs=[whole] * len(outs),
        scratch_shapes=list(scratch),
        compiler_params=pltpu.CompilerParams(vmem_limit_bytes=VMEM_BYTES),
        cost_estimate=pl.CostEstimate(flops=flops, bytes_accessed=moved, transcendentals=0),
    )(*args)


def struct(shape, dtype):
    return jax.ShapeDtypeStruct(shape, dtype)


def swap(array, axis, size, bit):
    return lax.ppermute(array, axis, [(i, i ^ bit) for i in range(size)])


def gather_columns(block, axis):
    size = lax.axis_size(axis)
    if size != 2:
        whole = lax.all_gather(block, axis, axis=1, tiled=True)
        return [whole], whole
    other = swap(block, axis, size, 1)
    first = lax.axis_index(axis) == 0
    return [block, other], jnp.concatenate(
        [jnp.where(first, block, other), jnp.where(first, other, block)], axis=1
    )


def turn(part):
    return call(transpose_kernel, [struct(part.shape[::-1], BF16)], (part,))[0]


def layer_grads(halves, inner, after):
    order = [0]
    bit = inner // 2
    while bit:
        order = order + [i ^ bit for i in order]
        bit //= 2
    turned = [turn(part) for part in halves]
    if inner == 1:
        return order, [[part] for part in turned]
    seq = lax.axis_size("seq")
    across = [swap(turned[0], "seq", seq, inner // 2)]
    if len(turned) == 2:
        late, _ = lax.optimization_barrier((across[0], after))
        across.append(swap(late, "tp", 2, 1))
    return order, [list(pair) for pair in zip(turned, across)]


def outer_kernel(at_ref, *refs, groups, tiles):
    *lhs_refs, rhs_ref, out_ref = refs
    count = len(lhs_refs) // groups
    depth = lhs_refs[0].shape[1]
    tile = at_ref[0] * pl.num_programs(0) + pl.program_id(0)
    for group in range(groups):

        @pl.when(tile // tiles == group)
        def _():
            total = 0.0
            for i, ref in enumerate(lhs_refs[group * count : (group + 1) * count]):
                total = total + matmul(ref[...], rhs_ref[pl.ds(i * depth, depth), :])
            out_ref[...] = total.astype(BF16)


def outer_product(groups, rhs, at, blocks):
    rows, depth = groups[0][0].shape
    size = rows * len(groups) // blocks
    tile = math.gcd(size, 512)
    tiles = rows // tile
    steps = size // tile
    wide = rhs.shape[1]

    def lhs_spec(group):
        return pl.BlockSpec(
            (tile, depth),
            lambda i, at_ref: (
                jnp.clip(at_ref[0] * steps + i - group * tiles, 0, tiles - 1),
                0,
            ),
        )

    flat = [part for group in groups for part in group]
    return pl.pallas_call(
        functools.partial(outer_kernel, groups=len(groups), tiles=tiles),
        grid_spec=pltpu.PrefetchScalarGridSpec(
            num_scalar_prefetch=1,
            grid=(steps,),
            in_specs=[lhs_spec(i) for i, group in enumerate(groups) for _ in group]
            + [pl.BlockSpec(rhs.shape, lambda i, at_ref: (0, 0))],
            out_specs=pl.BlockSpec((tile, wide), lambda i, at_ref: (i, 0)),
        ),
        out_shape=struct((size, wide), BF16),
        compiler_params=pltpu.CompilerParams(vmem_limit_bytes=VMEM_BYTES),
        cost_estimate=pl.CostEstimate(
            flops=4 * size * rhs.shape[0] * wide,
            bytes_accessed=2 * (len(groups[0]) * size * depth + size * wide),
            transcendentals=0,
        ),
    )(at.astype(jnp.int32)[None], *flat, rhs)


def halving_reduce_scatter(parts, size, inner, pieces):
    outer = len(parts)
    parts = list(parts)
    wide = parts[0].shape[1] // pieces
    cut = [slice(i * wide, (i + 1) * wide) for i in range(pieces)]
    before = None
    bit = 1
    while bit < outer:
        for d in reversed(range(bit, outer, 2 * bit)):
            sent = parts[d]
            if before is not None and d == bit and 2 * bit < outer:
                sent, _ = lax.optimization_barrier((sent, before))
            if 2 * bit < outer:
                before = moved = swap(sent, "seq", size, bit * inner)
                parts[d - bit] = parts[d - bit].astype(F32) + moved.astype(F32)
                if d > bit:
                    parts[d - bit] = parts[d - bit].astype(BF16)
            else:
                parts[0] = [
                    parts[0][:, c] + swap(sent[:, c], "seq", size, bit * inner).astype(F32)
                    for c in cut
                ]
        bit *= 2
    return parts[0] if outer > 1 else [parts[0][:, c] for c in cut]


def exchange(blocks, groups=None):
    return lax.all_to_all(
        blocks, "seq", split_axis=0, concat_axis=0, tiled=True, axis_index_groups=groups
    )


def on_device(values, gate, out_grad, out_weight, filt, decay):
    rows, width = values.shape
    seq = lax.axis_size("seq")
    me = lax.axis_index("seq")
    length = rows * seq
    own = width // seq
    norm_scale = 1.0 / math.sqrt(length)
    inner = 4 if seq % 4 == 0 else 1
    outer = seq // inner
    half = length // RADIX
    there, back = middle_tables(length)
    blocks = struct((seq, rows, own), BF16)
    spectrum = struct((half + 1, 2 * RADIX, 2 * own), F32)
    mid = pltpu.VMEM((half + 1, 2 * RADIX, 2 * own), BF16)
    work = 300 * (half + 1) * RADIX**2 * own
    start = (me * rows).astype(jnp.int32)[None]
    rates = decay[None, :]

    halves, full_grad = gather_columns(out_grad, "tp")
    (packed,) = call(
        functools.partial(pack_kernel, length=length),
        [struct((seq, 2, rows, own), BF16)],
        (values, filt, rates, start),
        scalar=(3,),
    )
    moved = exchange(packed)

    grad_y = jnp.dot(full_grad, out_weight, preferred_element_type=F32).astype(BF16)
    (gated_grad,) = call(gated_kernel, [struct((seq, 1, rows, own), BF16)], (grad_y, gate))
    gated_grad, moved = lax.optimization_barrier((gated_grad, moved))
    grad_c = exchange(gated_grad)

    spec, conv_out_c = call(
        conv_kernel,
        [spectrum, blocks],
        (moved, there, back),
        scratch=(mid,),
        flops=work,
    )
    place = (me % inner).astype(jnp.int32)[None]
    (gates,) = call(
        layer_pack_kernel, [struct((inner, outer, rows, own), BF16)], (gate, place), scalar=(1,)
    )
    gates, _ = lax.optimization_barrier((gates, moved))
    order, grads = layer_grads(halves, inner, conv_out_c)
    gates = [swap(gates[bit], "seq", seq, bit) if bit else gates[bit] for bit in order]
    conv_out_c, grad_c = lax.optimization_barrier((conv_out_c, grad_c))
    layers = [[z * inner + w for z in range(outer)] for w in range(inner)]
    conv_out = exchange(conv_out_c.reshape(outer, inner, rows, own), layers)

    conv_grad, kernel_grad = call(
        grad_kernel,
        [blocks, struct((seq, rows + STEP, own), BF16)],
        (grad_c, moved, spec, there, back),
        scratch=(mid,),
        flops=work,
    )
    flat, gates, _ = lax.optimization_barrier((sum(grads, []), gates, conv_grad))
    count = len(flat) // len(grads)
    grads = [flat[i : i + count] for i in range(0, len(flat), count)]
    bit = inner // 4
    while bit:
        grads = [g + [swap(part, "seq", seq, bit) for part in g] for g in grads]
        bit //= 2
    conv_grad, conv_out = lax.optimization_barrier((conv_grad, conv_out))
    conv_grad = exchange(conv_grad)

    block = struct((rows, width), BF16)
    home = struct((outer, rows, own), BF16)
    gated_out, *homes = call(
        functools.partial(layer_kernel, order=order),
        [struct((inner * rows, outer * own), BF16)] + [home] * inner,
        (*gates, conv_out, place),
        scalar=(inner + 1,),
    )
    shift = 0
    if len(grads) == 2:
        shift = lax.axis_index("tp") * (outer // 2)
    terms = [None] * outer
    for d in sorted(range(outer), key=lambda d: (-(d % 2), -d)):
        terms[d] = outer_product(grads, gated_out, (me // inner) ^ d ^ shift, outer)
        gated_out, _ = lax.optimization_barrier((gated_out, terms[d]))
    kernel_grad, conv_grad, _ = lax.optimization_barrier((kernel_grad, conv_grad, terms[1 % outer]))
    kernel_grad = exchange(kernel_grad)
    (d_values,) = call(values_kernel, [block], (conv_grad,))

    homes = {bit: swap(part, "seq", seq, bit) if bit else part for bit, part in zip(order, homes)}
    homes = jnp.stack([homes[bit] for bit in range(inner)])
    (d_gate,) = call(gate_kernel, [block], (homes, grad_y, place), scalar=(2,))
    d_filt, decay_grad = call(
        functools.partial(filt_kernel, length=length),
        [struct((rows, width), F32), struct((1, width), F32)],
        (kernel_grad, rates, start),
        scalar=(2,),
    )
    chunks = 2 if outer % 2 == 0 else 1
    wide = outer * own // chunks
    totals = halving_reduce_scatter(terms, seq, inner, chunks)
    totals[-1], d_gate, d_values = lax.optimization_barrier((totals[-1], d_gate, d_values))
    pieces = []
    for total in totals:
        total = total.astype(BF16).reshape(inner, -1, wide)
        for bit in range(inner):
            piece = lax.dynamic_index_in_dim(total, (me % inner) ^ bit, 0, keepdims=False)
            pieces.append(swap(piece, "seq", seq, bit) if bit else piece)
    pieces = jnp.stack(pieces).reshape(chunks, inner, -1, wide)
    (d_out_weight,) = call(
        functools.partial(weight_kernel, scale=norm_scale, own=own),
        [struct((pieces.shape[2], width), F32)],
        (pieces, place),
        scalar=(1,),
    )
    return (d_values, d_gate, d_filt, decay_grad[0], d_out_weight)


def solution(mesh):
    in_specs = (
        P("seq", "tp"),
        P("seq", "tp"),
        P("seq", "tp"),
        P(None, "tp"),
        P("seq", "tp"),
        P("tp"),
    )
    out_specs = (P("seq", "tp"), P("seq", "tp"), P("seq", "tp"), P("tp"), P("seq", "tp"))
    return jax.shard_map(
        on_device, mesh=mesh, in_specs=in_specs, out_specs=out_specs, check_vma=False
    )
```

```python
import functools
import math

import jax
import jax.numpy as jnp
import ml_dtypes
import numpy as np
from jax import lax
from jax.experimental import pallas as pl
from jax.experimental.pallas import tpu as pltpu
from jax.sharding import PartitionSpec as P

BF16 = jnp.bfloat16
F32 = jnp.float32
RADIX = 128
STEP = 16
VMEM_BYTES = 48 * 1024 * 1024


def middle_tables(length):
    padded = 2 * length
    outer = padded // RADIX
    k1 = np.arange(outer // 2 + 1)
    r = np.arange(RADIX)
    index = k1[:, None, None] * r[None, None, :] + outer * (r[:, None] * r[None, :])[None]
    phase = 2.0 * np.pi * (index % padded) / padded
    cos, sin = np.cos(phase), np.sin(phase)
    table = np.concatenate(
        [np.concatenate([cos, sin], axis=2), np.concatenate([-sin, cos], axis=2)], axis=1
    )
    there = jnp.asarray(table.astype(ml_dtypes.bfloat16))
    back = jnp.asarray(np.swapaxes(table, 1, 2).astype(ml_dtypes.bfloat16))
    return there, back


def real_forward(points):
    size = len(points)
    if size == 2:
        if points[1] is None:
            return [points[0], points[0]], [None, None]
        return [points[0] + points[1], points[0] - points[1]], [None, None]
    even_re, even_im = real_forward(points[0::2])
    odd_re, odd_im = real_forward(points[1::2])
    half = size // 2
    re, im = [None] * (half + 1), [None] * (half + 1)
    re[0], re[half] = even_re[0] + odd_re[0], even_re[0] - odd_re[0]
    for k in range(1, half // 2):
        cos = math.cos(2.0 * math.pi * k / size)
        sin = math.sin(2.0 * math.pi * k / size)
        turn_re = cos * odd_re[k] + sin * odd_im[k]
        turn_im = cos * odd_im[k] - sin * odd_re[k]
        re[k], im[k] = even_re[k] + turn_re, even_im[k] + turn_im
        re[half - k], im[half - k] = even_re[k] - turn_re, turn_im - even_im[k]
    re[half // 2], im[half // 2] = even_re[half // 2], -odd_re[half // 2]
    return re, im


def real_backward(re, im, wanted):
    half = len(re) - 1
    size = 2 * half
    if size == 2:
        return [re[0] + re[1]] + ([re[0] - re[1]] if wanted > 1 else [None])
    quarter = half // 2
    even_re, even_im = [None] * (quarter + 1), [None] * (quarter + 1)
    odd_re, odd_im = [None] * (quarter + 1), [None] * (quarter + 1)
    even_re[0], odd_re[0] = re[0] + re[half], re[0] - re[half]
    for k in range(1, quarter):
        cos = math.cos(2.0 * math.pi * k / size)
        sin = math.sin(2.0 * math.pi * k / size)
        even_re[k], even_im[k] = re[k] + re[half - k], im[k] - im[half - k]
        diff_re, diff_im = re[k] - re[half - k], im[k] + im[half - k]
        odd_re[k] = cos * diff_re - sin * diff_im
        odd_im[k] = cos * diff_im + sin * diff_re
    even_re[quarter], odd_re[quarter] = 2.0 * re[quarter], -2.0 * im[quarter]
    even = real_backward(even_re, even_im, wanted // 2)
    odd = real_backward(odd_re, odd_im, wanted // 2)
    return [point for pair in zip(even, odd) for point in pair]


def load_points(ref, chunk, half, field=0):
    per = ref.shape[2] // RADIX
    return [
        ref[p // per, field, pl.ds((p % per) * RADIX + chunk * STEP, STEP), :] for p in range(half)
    ]


def outer_forward(x_ref, mid_ref, lanes, field=0):
    half = mid_ref.shape[0] - 1

    def chunk_body(chunk, carry):
        points = [x.astype(F32) for x in load_points(x_ref, chunk, half, field)]
        re, im = real_forward(points + [None] * half)
        for k in range(half + 1):
            mid_ref[k, pl.ds(chunk * STEP, STEP), lanes] = re[k].astype(BF16)
            low = jnp.zeros_like(re[k]) if im[k] is None else im[k]
            mid_ref[k, pl.ds(RADIX + chunk * STEP, STEP), lanes] = low.astype(BF16)
        return carry

    lax.fori_loop(0, RADIX // STEP, chunk_body, 0)


def outer_backward(mid_ref, chunk, scale, lanes):
    half = mid_ref.shape[0] - 1
    re = [mid_ref[k, pl.ds(chunk * STEP, STEP), lanes].astype(F32) for k in range(half + 1)]
    im = [
        mid_ref[k, pl.ds(RADIX + chunk * STEP, STEP), lanes].astype(F32) if 0 < k < half else None
        for k in range(half + 1)
    ]
    return [scale * point for point in real_backward(re, im, half)[:half]]


def matmul(a, b):
    return jnp.dot(a, b, preferred_element_type=F32)


def product(a, b):
    a_re, a_im, b_re, b_im = a[:RADIX], a[RADIX:], b[:RADIX], b[RADIX:]
    return jnp.concatenate([a_re * b_re - a_im * b_im, a_re * b_im + a_im * b_re]).astype(BF16)


def conj_product(a, b):
    a_re, a_im, b_re, b_im = a[:RADIX], a[RADIX:], b[:RADIX], b[RADIX:]
    return jnp.concatenate([a_re * b_re + a_im * b_im, a_re * b_im - a_im * b_re]).astype(BF16)


def unrolled(count):
    return max(d for d in range(1, 14) if count % d == 0)


def conv_kernel(fields_ref, there_ref, back_ref, spec_ref, out_ref, mid):
    half = mid.shape[0] - 1
    own = out_ref.shape[2]
    low, high = slice(0, own), slice(own, 2 * own)
    scale = 0.5 / (half * RADIX)
    outer_forward(fields_ref, mid, low, 0)
    outer_forward(fields_ref, mid, high, 1)

    def freq_body(k, carry):
        spec = matmul(there_ref[k], mid[k])
        spec_ref[k] = spec
        mid[k, :, low] = matmul(back_ref[k], product(spec[:, low], spec[:, high])).astype(BF16)
        return carry

    lax.fori_loop(0, half + 1, freq_body, 0, unroll=unrolled(half + 1))
    per = out_ref.shape[1] // RADIX

    def chunk_body(chunk, carry):
        for p, point in enumerate(outer_backward(mid, chunk, scale, low)):
            rows = pl.ds((p % per) * RADIX + chunk * STEP, STEP)
            out_ref[p // per, rows, :] = point.astype(BF16)
        return carry

    lax.fori_loop(0, RADIX // STEP, chunk_body, 0)


def grad_kernel(g_ref, fields_ref, spec_ref, there_ref, back_ref, cg_ref, kg_ref, mid):
    half = mid.shape[0] - 1
    length = half * RADIX
    own = cg_ref.shape[2]
    low, high = slice(0, own), slice(own, 2 * own)
    scale = 0.5 / length
    outer_forward(g_ref, mid, low)

    def freq_body(k, carry):
        spec_g = matmul(there_ref[k], mid[k, :, low])
        both = jnp.concatenate([spec_g, spec_g], axis=1)
        mid[k] = matmul(back_ref[k], conj_product(spec_ref[k], both)).astype(BF16)
        return carry

    lax.fori_loop(0, half + 1, freq_body, 0, unroll=unrolled(half + 1))
    rows = g_ref.shape[2]
    per = rows // RADIX

    def chunk_body(chunk, total):
        for p, point in enumerate(outer_backward(mid, chunk, scale, high)):
            here = pl.ds((p % per) * RADIX + chunk * STEP, STEP)
            cg_ref[p // per, here, :] = point.astype(BF16)
        kernel = load_points(fields_ref, chunk, half, 1)
        first = lax.broadcasted_iota(jnp.int32, total.shape, 0) + chunk * STEP
        for p, point in enumerate(outer_backward(mid, chunk, scale, low)):
            here = pl.ds((p % per) * RADIX + chunk * STEP, STEP)
            kg_ref[p // per, here, :] = point.astype(BF16)
            place = (first + p * RADIX).astype(F32) * (1.0 / length)
            total = total + place * point * kernel[p].astype(F32)
        return total

    total = jnp.zeros((STEP, own), F32)
    total = lax.fori_loop(0, RADIX // STEP, chunk_body, total)
    total = -(1.0 / math.sqrt(length)) * jnp.sum(total, axis=0, keepdims=True)
    leading = total.astype(BF16).astype(F32)
    row = lax.broadcasted_iota(jnp.int32, (STEP, own), 0)
    extra = jnp.where(row == 0, leading, jnp.where(row == 1, total - leading, 0.0)).astype(BF16)
    for device in range(kg_ref.shape[0]):
        kg_ref[device, pl.ds(rows, STEP), :] = extra


def pack_kernel(v_ref, filt_ref, decay_ref, start_ref, out_ref, *, length):
    own = out_ref.shape[3]
    rows = v_ref.shape[0]
    row = lax.broadcasted_iota(jnp.int32, (rows, own), 0) + start_ref[0]
    position = row.astype(F32) * (1.0 / length)
    for d in range(out_ref.shape[0]):
        cols = slice(d * own, (d + 1) * own)
        out_ref[d, 0] = v_ref[:, cols]
        window = jnp.exp(-decay_ref[:, cols] * position)
        out_ref[d, 1] = (filt_ref[:, cols] * window * (1.0 / math.sqrt(length))).astype(BF16)


def gated_kernel(grad_ref, gate_ref, out_ref):
    own = out_ref.shape[3]
    for d in range(out_ref.shape[0]):
        cols = slice(d * own, (d + 1) * own)
        out_ref[d, 0] = (grad_ref[:, cols].astype(F32) * gate_ref[:, cols].astype(F32)).astype(BF16)


def layer_pack_kernel(gate_ref, place_ref, out_ref):
    inner, outer, _, own = out_ref.shape
    for z in range(outer):
        for w in range(inner):
            first = (z * inner + w) * own
            out_ref[place_ref[0] ^ w, z] = gate_ref[:, slice(first, first + own)]


def layer_kernel(*refs, order):
    count = len(order)
    gates, homes = refs[:count], refs[count + 3 :]
    moved_ref, place_ref, gated_ref = refs[count : count + 3]
    outer, _, rows, own = moved_ref.shape
    for i, bit in enumerate(order):
        for z in range(outer):
            conv_out = moved_ref[z, place_ref[0] ^ bit]
            homes[i][z] = conv_out
            gated = (gates[i][z].astype(F32) * conv_out.astype(F32)).astype(BF16)
            gated_ref[pl.ds(i * rows, rows), slice(z * own, (z + 1) * own)] = gated


def gate_kernel(moved_ref, grad_ref, place_ref, out_ref):
    inner, outer, _, own = moved_ref.shape
    for z in range(outer):
        for w in range(inner):
            cols = slice((z * inner + w) * own, (z * inner + w + 1) * own)
            conv_out = moved_ref[place_ref[0] ^ w, z].astype(F32)
            out_ref[:, cols] = (grad_ref[:, cols].astype(F32) * conv_out).astype(BF16)


def weight_kernel(moved_ref, place_ref, out_ref, *, scale, own):
    chunks, inner, _, wide = moved_ref.shape
    per = wide // own
    for z in range(chunks * per):
        for w in range(inner):
            cols = slice((z * inner + w) * own, (z * inner + w + 1) * own)
            first = (z % per) * own
            part = moved_ref[z // per, place_ref[0] ^ w, :, slice(first, first + own)]
            out_ref[:, cols] = part.astype(F32) * scale


def transpose_kernel(x_ref, out_ref):
    rows = x_ref.shape[0]
    for first in range(0, x_ref.shape[1], rows):
        out_ref[pl.ds(first, rows), :] = x_ref[:, slice(first, first + rows)].T


def values_kernel(moved_ref, out_ref):
    own = moved_ref.shape[2]
    for d in range(moved_ref.shape[0]):
        out_ref[:, slice(d * own, (d + 1) * own)] = moved_ref[d]


def filt_kernel(moved_ref, decay_ref, start_ref, d_filt_ref, decay_grad_ref, *, length):
    own = moved_ref.shape[2]
    rows = d_filt_ref.shape[0]
    row = lax.broadcasted_iota(jnp.int32, (rows, own), 0) + start_ref[0]
    position = row.astype(F32) * (1.0 / length)
    for d in range(moved_ref.shape[0]):
        cols = slice(d * own, (d + 1) * own)
        window = jnp.exp(-decay_ref[:, cols] * position)
        kernel_grad = moved_ref[d, pl.ds(0, rows), :].astype(F32)
        d_filt_ref[:, cols] = kernel_grad * window * (1.0 / math.sqrt(length))
        extra = moved_ref[d, pl.ds(rows, STEP), :].astype(F32)
        decay_grad_ref[:, cols] = extra[0:1] + extra[1:2]


def call(kernel, outs, args, scratch=(), flops=0, scalar=()):
    whole = pl.BlockSpec(memory_space=pltpu.VMEM)
    specs = [
        pl.BlockSpec(memory_space=pltpu.SMEM) if i in scalar else whole for i in range(len(args))
    ]
    moved = sum(math.prod(a.shape) * a.dtype.itemsize for a in (*args, *outs))
    return pl.pallas_call(
        kernel,
        out_shape=outs,
        in_specs=specs,
        out_specs=[whole] * len(outs),
        scratch_shapes=list(scratch),
        compiler_params=pltpu.CompilerParams(vmem_limit_bytes=VMEM_BYTES),
        cost_estimate=pl.CostEstimate(flops=flops, bytes_accessed=moved, transcendentals=0),
    )(*args)


def struct(shape, dtype):
    return jax.ShapeDtypeStruct(shape, dtype)


def swap(array, axis, size, bit):
    return lax.ppermute(array, axis, [(i, i ^ bit) for i in range(size)])


def gather_columns(block, axis):
    size = lax.axis_size(axis)
    if size != 2:
        whole = lax.all_gather(block, axis, axis=1, tiled=True)
        return [whole], whole
    other = swap(block, axis, size, 1)
    first = lax.axis_index(axis) == 0
    return [block, other], jnp.concatenate(
        [jnp.where(first, block, other), jnp.where(first, other, block)], axis=1
    )


def turn(part):
    return call(transpose_kernel, [struct(part.shape[::-1], BF16)], (part,))[0]


def layer_grads(halves, inner):
    order = [0]
    bit = inner // 2
    while bit:
        order = order + [i ^ bit for i in order]
        bit //= 2
    turned = [turn(part) for part in halves]
    across = []
    if inner > 1:
        across = [swap(turned[0], "seq", lax.axis_size("seq"), inner // 2)]
    return order, turned, across


def outer_kernel(at_ref, *refs, groups, tiles):
    *lhs_refs, rhs_ref, out_ref = refs
    count = len(lhs_refs) // groups
    depth = lhs_refs[0].shape[1]
    tile = at_ref[0] * pl.num_programs(0) + pl.program_id(0)
    for group in range(groups):

        @pl.when(tile // tiles == group)
        def _():
            total = 0.0
            for i, ref in enumerate(lhs_refs[group * count : (group + 1) * count]):
                total = total + matmul(ref[...], rhs_ref[pl.ds(i * depth, depth), :])
            out_ref[...] = total.astype(BF16)


def outer_product(groups, rhs, at, blocks):
    rows, depth = groups[0][0].shape
    size = rows * len(groups) // blocks
    tile = math.gcd(size, 512)
    tiles = rows // tile
    steps = size // tile
    wide = rhs.shape[1]

    def lhs_spec(group):
        return pl.BlockSpec(
            (tile, depth),
            lambda i, at_ref: (
                jnp.clip(at_ref[0] * steps + i - group * tiles, 0, tiles - 1),
                0,
            ),
        )

    flat = [part for group in groups for part in group]
    return pl.pallas_call(
        functools.partial(outer_kernel, groups=len(groups), tiles=tiles),
        grid_spec=pltpu.PrefetchScalarGridSpec(
            num_scalar_prefetch=1,
            grid=(steps,),
            in_specs=[lhs_spec(i) for i, group in enumerate(groups) for _ in group]
            + [pl.BlockSpec(rhs.shape, lambda i, at_ref: (0, 0))],
            out_specs=pl.BlockSpec((tile, wide), lambda i, at_ref: (i, 0)),
        ),
        out_shape=struct((size, wide), BF16),
        compiler_params=pltpu.CompilerParams(vmem_limit_bytes=VMEM_BYTES),
        cost_estimate=pl.CostEstimate(
            flops=4 * size * rhs.shape[0] * wide,
            bytes_accessed=2 * (len(groups[0]) * size * depth + size * wide),
            transcendentals=0,
        ),
    )(at.astype(jnp.int32)[None], *flat, rhs)


def halving_reduce_scatter(parts, size, inner, pieces, beside, late):
    outer = len(parts)
    parts = list(parts)
    wide = parts[0].shape[1] // pieces
    cut = [slice(i * wide, (i + 1) * wide) for i in range(pieces)]
    before = None
    bit = 1
    while bit < outer:
        for d in reversed(range(bit, outer, 2 * bit)):
            sent = parts[d]
            if before is not None and d == bit and 2 * bit < outer:
                sent, _ = lax.optimization_barrier((sent, before))
            if 2 * bit < outer:
                moved = swap(sent, "seq", size, bit * inner)
                if before is None:
                    moved, beside = lax.optimization_barrier((moved, beside))
                elif d == 1:
                    moved, late = lax.optimization_barrier((moved, late))
                before = moved
                parts[d - bit] = parts[d - bit].astype(F32) + moved.astype(F32)
                if d > bit:
                    parts[d - bit] = parts[d - bit].astype(BF16)
            else:
                parts[0] = [
                    parts[0][:, c] + swap(sent[:, c], "seq", size, bit * inner).astype(F32)
                    for c in cut
                ]
        bit *= 2
    if outer == 1:
        parts[0] = [parts[0][:, c] for c in cut]
    return parts[0], beside, late


def exchange(blocks, groups=None):
    return lax.all_to_all(
        blocks, "seq", split_axis=0, concat_axis=0, tiled=True, axis_index_groups=groups
    )


def on_device(values, gate, out_grad, out_weight, filt, decay):
    rows, width = values.shape
    seq = lax.axis_size("seq")
    me = lax.axis_index("seq")
    length = rows * seq
    own = width // seq
    norm_scale = 1.0 / math.sqrt(length)
    inner = 4 if seq % 4 == 0 else 1
    outer = seq // inner
    half = length // RADIX
    there, back = middle_tables(length)
    blocks = struct((seq, rows, own), BF16)
    spectrum = struct((half + 1, 2 * RADIX, 2 * own), F32)
    mid = pltpu.VMEM((half + 1, 2 * RADIX, 2 * own), BF16)
    work = 300 * (half + 1) * RADIX**2 * own
    start = (me * rows).astype(jnp.int32)[None]
    rates = decay[None, :]

    halves, full_grad = gather_columns(out_grad, "tp")
    (packed,) = call(
        functools.partial(pack_kernel, length=length),
        [struct((seq, 2, rows, own), BF16)],
        (values, filt, rates, start),
        scalar=(3,),
    )
    moved = exchange(packed)

    grad_y = jnp.dot(full_grad, out_weight, preferred_element_type=F32).astype(BF16)
    (gated_grad,) = call(gated_kernel, [struct((seq, 1, rows, own), BF16)], (grad_y, gate))
    gated_grad, moved = lax.optimization_barrier((gated_grad, moved))
    grad_c = exchange(gated_grad)

    place = (me % inner).astype(jnp.int32)[None]
    (gates,) = call(
        layer_pack_kernel, [struct((inner, outer, rows, own), BF16)], (gate, place), scalar=(1,)
    )
    gates, _ = lax.optimization_barrier((gates, moved))
    order, turned, across = layer_grads(halves, inner)
    if across:
        across[0], *turned, moved = lax.optimization_barrier((across[0], *turned, moved))
    spec, conv_out_c = call(
        conv_kernel,
        [spectrum, blocks],
        (moved, there, back),
        scratch=(mid,),
        flops=work,
    )
    if len(turned) == 2 and across:
        late, _ = lax.optimization_barrier((across[0], conv_out_c))
        across.append(swap(late, "tp", 2, 1))
    grads = [list(pair) for pair in (zip(turned, across) if across else zip(turned))]
    gates = [swap(gates[bit], "seq", seq, bit) if bit else gates[bit] for bit in order]
    conv_out_c, grad_c = lax.optimization_barrier((conv_out_c, grad_c))
    layers = [[z * inner + w for z in range(outer)] for w in range(inner)]
    conv_out = exchange(conv_out_c.reshape(outer, inner, rows, own), layers)

    *gates, grad_c = lax.optimization_barrier((*gates, grad_c))
    conv_grad, kernel_grad = call(
        grad_kernel,
        [blocks, struct((seq, rows + STEP, own), BF16)],
        (grad_c, moved, spec, there, back),
        scratch=(mid,),
        flops=work,
    )
    flat, gates, _ = lax.optimization_barrier((sum(grads, []), gates, conv_grad))
    count = len(flat) // len(grads)
    grads = [flat[i : i + count] for i in range(0, len(flat), count)]
    bit = inner // 4
    while bit:
        grads = [g + [swap(part, "seq", seq, bit) for part in g] for g in grads]
        bit //= 2
    conv_grad, conv_out = lax.optimization_barrier((conv_grad, conv_out))
    conv_grad = exchange(conv_grad)

    block = struct((rows, width), BF16)
    home = struct((outer, rows, own), BF16)
    gated_out, *homes = call(
        functools.partial(layer_kernel, order=order),
        [struct((inner * rows, outer * own), BF16)] + [home] * inner,
        (*gates, conv_out, place),
        scalar=(inner + 1,),
    )
    shift = 0
    if len(grads) == 2:
        shift = lax.axis_index("tp") * (outer // 2)
    terms = [None] * outer
    for d in sorted(range(outer), key=lambda d: (-(d % 2), -d)):
        terms[d] = outer_product(grads, gated_out, (me // inner) ^ d ^ shift, outer)
        gated_out, _ = lax.optimization_barrier((gated_out, terms[d]))
    kernel_grad, conv_grad, _ = lax.optimization_barrier((kernel_grad, conv_grad, terms[1 % outer]))
    kernel_grad = exchange(kernel_grad)

    homes = {bit: swap(part, "seq", seq, bit) if bit else part for bit, part in zip(order, homes)}
    homes = jnp.stack([homes[bit] for bit in range(inner)])
    (d_gate,) = call(gate_kernel, [block], (homes, grad_y, place), scalar=(2,))
    chunks = 1
    wide = outer * own // chunks
    totals, conv_grad, kernel_grad = halving_reduce_scatter(
        terms, seq, inner, chunks, conv_grad, kernel_grad
    )
    (d_values,) = call(values_kernel, [block], (conv_grad,))
    d_filt, decay_grad = call(
        functools.partial(filt_kernel, length=length),
        [struct((rows, width), F32), struct((1, width), F32)],
        (kernel_grad, rates, start),
        scalar=(2,),
    )
    totals[-1], d_gate, d_values = lax.optimization_barrier((totals[-1], d_gate, d_values))
    pieces = []
    for total in totals:
        total = total.astype(BF16).reshape(inner, -1, wide)
        for bit in range(inner):
            piece = lax.dynamic_index_in_dim(total, (me % inner) ^ bit, 0, keepdims=False)
            pieces.append(swap(piece, "seq", seq, bit) if bit else piece)
    pieces = jnp.stack(pieces).reshape(chunks, inner, -1, wide)
    (d_out_weight,) = call(
        functools.partial(weight_kernel, scale=norm_scale, own=own),
        [struct((pieces.shape[2], width), F32)],
        (pieces, place),
        scalar=(1,),
    )
    return (d_values, d_gate, d_filt, decay_grad[0], d_out_weight)


def solution(mesh):
    in_specs = (
        P("seq", "tp"),
        P("seq", "tp"),
        P("seq", "tp"),
        P(None, "tp"),
        P("seq", "tp"),
        P("tp"),
    )
    out_specs = (P("seq", "tp"), P("seq", "tp"), P("seq", "tp"), P("tp"), P("seq", "tp"))
    return jax.shard_map(
        on_device, mesh=mesh, in_specs=in_specs, out_specs=out_specs, check_vma=False
    )
```

```python
import functools
import math

import jax
import jax.numpy as jnp
import ml_dtypes
import numpy as np
from jax import lax
from jax.experimental import pallas as pl
from jax.experimental.pallas import tpu as pltpu
from jax.sharding import PartitionSpec as P

BF16 = jnp.bfloat16
F32 = jnp.float32
RADIX = 128
STEP = 16
VMEM_BYTES = 48 * 1024 * 1024


def middle_tables(length):
    padded = 2 * length
    outer = padded // RADIX
    k1 = np.arange(outer // 2 + 1)
    r = np.arange(RADIX)
    index = k1[:, None, None] * r[None, None, :] + outer * (r[:, None] * r[None, :])[None]
    phase = 2.0 * np.pi * (index % padded) / padded
    cos, sin = np.cos(phase), np.sin(phase)
    table = np.concatenate(
        [np.concatenate([cos, sin], axis=2), np.concatenate([-sin, cos], axis=2)], axis=1
    )
    there = jnp.asarray(table.astype(ml_dtypes.bfloat16))
    back = jnp.asarray(np.swapaxes(table, 1, 2).astype(ml_dtypes.bfloat16))
    return there, back


def real_forward(points):
    size = len(points)
    if size == 2:
        if points[1] is None:
            return [points[0], points[0]], [None, None]
        return [points[0] + points[1], points[0] - points[1]], [None, None]
    even_re, even_im = real_forward(points[0::2])
    odd_re, odd_im = real_forward(points[1::2])
    half = size // 2
    re, im = [None] * (half + 1), [None] * (half + 1)
    re[0], re[half] = even_re[0] + odd_re[0], even_re[0] - odd_re[0]
    for k in range(1, half // 2):
        cos = math.cos(2.0 * math.pi * k / size)
        sin = math.sin(2.0 * math.pi * k / size)
        turn_re = cos * odd_re[k] + sin * odd_im[k]
        turn_im = cos * odd_im[k] - sin * odd_re[k]
        re[k], im[k] = even_re[k] + turn_re, even_im[k] + turn_im
        re[half - k], im[half - k] = even_re[k] - turn_re, turn_im - even_im[k]
    re[half // 2], im[half // 2] = even_re[half // 2], -odd_re[half // 2]
    return re, im


def real_backward(re, im, wanted):
    half = len(re) - 1
    size = 2 * half
    if size == 2:
        return [re[0] + re[1]] + ([re[0] - re[1]] if wanted > 1 else [None])
    quarter = half // 2
    even_re, even_im = [None] * (quarter + 1), [None] * (quarter + 1)
    odd_re, odd_im = [None] * (quarter + 1), [None] * (quarter + 1)
    even_re[0], odd_re[0] = re[0] + re[half], re[0] - re[half]
    for k in range(1, quarter):
        cos = math.cos(2.0 * math.pi * k / size)
        sin = math.sin(2.0 * math.pi * k / size)
        even_re[k], even_im[k] = re[k] + re[half - k], im[k] - im[half - k]
        diff_re, diff_im = re[k] - re[half - k], im[k] + im[half - k]
        odd_re[k] = cos * diff_re - sin * diff_im
        odd_im[k] = cos * diff_im + sin * diff_re
    even_re[quarter], odd_re[quarter] = 2.0 * re[quarter], -2.0 * im[quarter]
    even = real_backward(even_re, even_im, wanted // 2)
    odd = real_backward(odd_re, odd_im, wanted // 2)
    return [point for pair in zip(even, odd) for point in pair]


def load_points(ref, chunk, half, field=0):
    per = ref.shape[2] // RADIX
    return [
        ref[p // per, field, pl.ds((p % per) * RADIX + chunk * STEP, STEP), :] for p in range(half)
    ]


def outer_forward(x_ref, mid_ref, lanes, field=0):
    half = mid_ref.shape[0] - 1

    def chunk_body(chunk, carry):
        points = [x.astype(F32) for x in load_points(x_ref, chunk, half, field)]
        re, im = real_forward(points + [None] * half)
        for k in range(half + 1):
            mid_ref[k, pl.ds(chunk * STEP, STEP), lanes] = re[k].astype(BF16)
            low = jnp.zeros_like(re[k]) if im[k] is None else im[k]
            mid_ref[k, pl.ds(RADIX + chunk * STEP, STEP), lanes] = low.astype(BF16)
        return carry

    lax.fori_loop(0, RADIX // STEP, chunk_body, 0)


def outer_backward(mid_ref, chunk, scale, lanes):
    half = mid_ref.shape[0] - 1
    re = [mid_ref[k, pl.ds(chunk * STEP, STEP), lanes].astype(F32) for k in range(half + 1)]
    im = [
        mid_ref[k, pl.ds(RADIX + chunk * STEP, STEP), lanes].astype(F32) if 0 < k < half else None
        for k in range(half + 1)
    ]
    return [scale * point for point in real_backward(re, im, half)[:half]]


def matmul(a, b):
    return jnp.dot(a, b, preferred_element_type=F32)


def product(a, b):
    a_re, a_im, b_re, b_im = a[:RADIX], a[RADIX:], b[:RADIX], b[RADIX:]
    return jnp.concatenate([a_re * b_re - a_im * b_im, a_re * b_im + a_im * b_re]).astype(BF16)


def conj_product(a, b):
    a_re, a_im, b_re, b_im = a[:RADIX], a[RADIX:], b[:RADIX], b[RADIX:]
    return jnp.concatenate([a_re * b_re + a_im * b_im, a_re * b_im - a_im * b_re]).astype(BF16)


def unrolled(count):
    return max(d for d in range(1, 14) if count % d == 0)


def conv_kernel(fields_ref, there_ref, back_ref, spec_ref, out_ref, mid):
    half = mid.shape[0] - 1
    own = out_ref.shape[2]
    low, high = slice(0, own), slice(own, 2 * own)
    scale = 0.5 / (half * RADIX)
    outer_forward(fields_ref, mid, low, 0)
    outer_forward(fields_ref, mid, high, 1)

    def freq_body(k, carry):
        spec = matmul(there_ref[k], mid[k])
        spec_ref[k] = spec
        mid[k, :, low] = matmul(back_ref[k], product(spec[:, low], spec[:, high])).astype(BF16)
        return carry

    lax.fori_loop(0, half + 1, freq_body, 0, unroll=unrolled(half + 1))
    per = out_ref.shape[1] // RADIX

    def chunk_body(chunk, carry):
        for p, point in enumerate(outer_backward(mid, chunk, scale, low)):
            rows = pl.ds((p % per) * RADIX + chunk * STEP, STEP)
            out_ref[p // per, rows, :] = point.astype(BF16)
        return carry

    lax.fori_loop(0, RADIX // STEP, chunk_body, 0)


def grad_kernel(g_ref, fields_ref, spec_ref, there_ref, back_ref, cg_ref, kg_ref, mid):
    half = mid.shape[0] - 1
    length = half * RADIX
    own = cg_ref.shape[2]
    low, high = slice(0, own), slice(own, 2 * own)
    scale = 0.5 / length
    outer_forward(g_ref, mid, low)

    def freq_body(k, carry):
        spec_g = matmul(there_ref[k], mid[k, :, low])
        both = jnp.concatenate([spec_g, spec_g], axis=1)
        mid[k] = matmul(back_ref[k], conj_product(spec_ref[k], both)).astype(BF16)
        return carry

    lax.fori_loop(0, half + 1, freq_body, 0, unroll=unrolled(half + 1))
    rows = g_ref.shape[2]
    per = rows // RADIX

    def chunk_body(chunk, total):
        for p, point in enumerate(outer_backward(mid, chunk, scale, high)):
            here = pl.ds((p % per) * RADIX + chunk * STEP, STEP)
            cg_ref[p // per, here, :] = point.astype(BF16)
        kernel = load_points(fields_ref, chunk, half, 1)
        first = lax.broadcasted_iota(jnp.int32, total.shape, 0) + chunk * STEP
        for p, point in enumerate(outer_backward(mid, chunk, scale, low)):
            here = pl.ds((p % per) * RADIX + chunk * STEP, STEP)
            kg_ref[p // per, here, :] = point.astype(BF16)
            place = (first + p * RADIX).astype(F32) * (1.0 / length)
            total = total + place * point * kernel[p].astype(F32)
        return total

    total = jnp.zeros((STEP, own), F32)
    total = lax.fori_loop(0, RADIX // STEP, chunk_body, total)
    total = -(1.0 / math.sqrt(length)) * jnp.sum(total, axis=0, keepdims=True)
    leading = total.astype(BF16).astype(F32)
    row = lax.broadcasted_iota(jnp.int32, (STEP, own), 0)
    extra = jnp.where(row == 0, leading, jnp.where(row == 1, total - leading, 0.0)).astype(BF16)
    for device in range(kg_ref.shape[0]):
        kg_ref[device, pl.ds(rows, STEP), :] = extra


def pack_kernel(v_ref, filt_ref, decay_ref, start_ref, out_ref, *, length):
    own = out_ref.shape[3]
    rows = v_ref.shape[0]
    row = lax.broadcasted_iota(jnp.int32, (rows, own), 0) + start_ref[0]
    position = row.astype(F32) * (1.0 / length)
    for d in range(out_ref.shape[0]):
        cols = slice(d * own, (d + 1) * own)
        out_ref[d, 0] = v_ref[:, cols]
        window = jnp.exp(-decay_ref[:, cols] * position)
        out_ref[d, 1] = (filt_ref[:, cols] * window * (1.0 / math.sqrt(length))).astype(BF16)


def gated_kernel(grad_ref, gate_ref, out_ref):
    own = out_ref.shape[3]
    for d in range(out_ref.shape[0]):
        cols = slice(d * own, (d + 1) * own)
        out_ref[d, 0] = (grad_ref[:, cols].astype(F32) * gate_ref[:, cols].astype(F32)).astype(BF16)


def layer_pack_kernel(gate_ref, place_ref, out_ref):
    inner, outer, _, own = out_ref.shape
    for z in range(outer):
        for w in range(inner):
            first = (z * inner + w) * own
            out_ref[place_ref[0] ^ w, z] = gate_ref[:, slice(first, first + own)]


def layer_kernel(*refs, order):
    count = len(order)
    gates, homes = refs[:count], refs[count + 3 :]
    moved_ref, place_ref, gated_ref = refs[count : count + 3]
    outer, _, rows, own = moved_ref.shape
    for i, bit in enumerate(order):
        for z in range(outer):
            conv_out = moved_ref[z, place_ref[0] ^ bit]
            homes[i][z] = conv_out
            gated = (gates[i][z].astype(F32) * conv_out.astype(F32)).astype(BF16)
            gated_ref[pl.ds(i * rows, rows), slice(z * own, (z + 1) * own)] = gated


def gate_kernel(moved_ref, grad_ref, place_ref, out_ref):
    inner, outer, _, own = moved_ref.shape
    for z in range(outer):
        for w in range(inner):
            cols = slice((z * inner + w) * own, (z * inner + w + 1) * own)
            conv_out = moved_ref[place_ref[0] ^ w, z].astype(F32)
            out_ref[:, cols] = (grad_ref[:, cols].astype(F32) * conv_out).astype(BF16)


def weight_kernel(moved_ref, place_ref, out_ref, *, scale, own):
    chunks, inner, _, wide = moved_ref.shape
    per = wide // own
    for z in range(chunks * per):
        for w in range(inner):
            cols = slice((z * inner + w) * own, (z * inner + w + 1) * own)
            first = (z % per) * own
            part = moved_ref[z // per, place_ref[0] ^ w, :, slice(first, first + own)]
            out_ref[:, cols] = part.astype(F32) * scale


def transpose_kernel(x_ref, out_ref):
    rows = x_ref.shape[0]
    for first in range(0, x_ref.shape[1], rows):
        out_ref[pl.ds(first, rows), :] = x_ref[:, slice(first, first + rows)].T


def values_kernel(moved_ref, out_ref):
    own = moved_ref.shape[2]
    for d in range(moved_ref.shape[0]):
        out_ref[:, slice(d * own, (d + 1) * own)] = moved_ref[d]


def filt_kernel(moved_ref, decay_ref, start_ref, d_filt_ref, decay_grad_ref, *, length):
    own = moved_ref.shape[2]
    rows = d_filt_ref.shape[0]
    row = lax.broadcasted_iota(jnp.int32, (rows, own), 0) + start_ref[0]
    position = row.astype(F32) * (1.0 / length)
    for d in range(moved_ref.shape[0]):
        cols = slice(d * own, (d + 1) * own)
        window = jnp.exp(-decay_ref[:, cols] * position)
        kernel_grad = moved_ref[d, pl.ds(0, rows), :].astype(F32)
        d_filt_ref[:, cols] = kernel_grad * window * (1.0 / math.sqrt(length))
        extra = moved_ref[d, pl.ds(rows, STEP), :].astype(F32)
        decay_grad_ref[:, cols] = extra[0:1] + extra[1:2]


def call(kernel, outs, args, scratch=(), flops=0, scalar=()):
    whole = pl.BlockSpec(memory_space=pltpu.VMEM)
    specs = [
        pl.BlockSpec(memory_space=pltpu.SMEM) if i in scalar else whole for i in range(len(args))
    ]
    moved = sum(math.prod(a.shape) * a.dtype.itemsize for a in (*args, *outs))
    return pl.pallas_call(
        kernel,
        out_shape=outs,
        in_specs=specs,
        out_specs=[whole] * len(outs),
        scratch_shapes=list(scratch),
        compiler_params=pltpu.CompilerParams(vmem_limit_bytes=VMEM_BYTES),
        cost_estimate=pl.CostEstimate(flops=flops, bytes_accessed=moved, transcendentals=0),
    )(*args)


def struct(shape, dtype):
    return jax.ShapeDtypeStruct(shape, dtype)


def swap(array, axis, size, bit):
    return lax.ppermute(array, axis, [(i, i ^ bit) for i in range(size)])


def gather_columns(block, axis):
    size = lax.axis_size(axis)
    if size != 2:
        whole = lax.all_gather(block, axis, axis=1, tiled=True)
        return [whole], whole
    other = swap(block, axis, size, 1)
    first = lax.axis_index(axis) == 0
    return [block, other], jnp.concatenate(
        [jnp.where(first, block, other), jnp.where(first, other, block)], axis=1
    )


def turn(part):
    return call(transpose_kernel, [struct(part.shape[::-1], BF16)], (part,))[0]


def layer_grads(halves, inner):
    order = [0]
    bit = inner // 2
    while bit:
        order = order + [i ^ bit for i in order]
        bit //= 2
    turned = [turn(part) for part in halves]
    across = []
    if inner > 1:
        across = [swap(turned[0], "seq", lax.axis_size("seq"), inner // 2)]
    return order, turned, across


def outer_kernel(at_ref, *refs, groups, tiles):
    *lhs_refs, rhs_ref, out_ref = refs
    count = len(lhs_refs) // groups
    depth = lhs_refs[0].shape[1]
    tile = at_ref[0] * pl.num_programs(0) + pl.program_id(0)
    for group in range(groups):

        @pl.when(tile // tiles == group)
        def _():
            total = 0.0
            for i, ref in enumerate(lhs_refs[group * count : (group + 1) * count]):
                total = total + matmul(ref[...], rhs_ref[pl.ds(i * depth, depth), :])
            out_ref[...] = total.astype(BF16)


def outer_product(groups, rhs, at, blocks):
    rows, depth = groups[0][0].shape
    size = rows * len(groups) // blocks
    tile = math.gcd(size, 1024)
    tiles = rows // tile
    steps = size // tile
    wide = rhs.shape[1]

    def lhs_spec(group):
        return pl.BlockSpec(
            (tile, depth),
            lambda i, at_ref: (
                jnp.clip(at_ref[0] * steps + i - group * tiles, 0, tiles - 1),
                0,
            ),
        )

    flat = [part for group in groups for part in group]
    return pl.pallas_call(
        functools.partial(outer_kernel, groups=len(groups), tiles=tiles),
        grid_spec=pltpu.PrefetchScalarGridSpec(
            num_scalar_prefetch=1,
            grid=(steps,),
            in_specs=[lhs_spec(i) for i, group in enumerate(groups) for _ in group]
            + [pl.BlockSpec(rhs.shape, lambda i, at_ref: (0, 0))],
            out_specs=pl.BlockSpec((tile, wide), lambda i, at_ref: (i, 0)),
        ),
        out_shape=struct((size, wide), BF16),
        compiler_params=pltpu.CompilerParams(vmem_limit_bytes=VMEM_BYTES),
        cost_estimate=pl.CostEstimate(
            flops=4 * size * rhs.shape[0] * wide,
            bytes_accessed=2 * (len(groups[0]) * size * depth + size * wide),
            transcendentals=0,
        ),
    )(at.astype(jnp.int32)[None], *flat, rhs)


def halving_reduce_scatter(parts, size, inner, pieces, beside, late):
    outer = len(parts)
    parts = list(parts)
    wide = parts[0].shape[1] // pieces
    cut = [slice(i * wide, (i + 1) * wide) for i in range(pieces)]
    before = None
    bit = 1
    while bit < outer:
        for d in reversed(range(bit, outer, 2 * bit)):
            sent = parts[d]
            if before is not None and d == bit and 2 * bit < outer:
                sent, _ = lax.optimization_barrier((sent, before))
            if 2 * bit < outer:
                moved = swap(sent, "seq", size, bit * inner)
                if before is None:
                    moved, beside = lax.optimization_barrier((moved, beside))
                elif d == 1:
                    moved, late = lax.optimization_barrier((moved, late))
                before = moved
                parts[d - bit] = parts[d - bit].astype(F32) + moved.astype(F32)
                if d > bit:
                    parts[d - bit] = parts[d - bit].astype(BF16)
            else:
                parts[0] = [
                    parts[0][:, c] + swap(sent[:, c], "seq", size, bit * inner).astype(F32)
                    for c in cut
                ]
        bit *= 2
    if outer == 1:
        parts[0] = [parts[0][:, c] for c in cut]
    return parts[0], beside, late


def exchange(blocks, groups=None):
    return lax.all_to_all(
        blocks, "seq", split_axis=0, concat_axis=0, tiled=True, axis_index_groups=groups
    )


def on_device(values, gate, out_grad, out_weight, filt, decay):
    rows, width = values.shape
    seq = lax.axis_size("seq")
    me = lax.axis_index("seq")
    length = rows * seq
    own = width // seq
    norm_scale = 1.0 / math.sqrt(length)
    inner = 4 if seq % 4 == 0 else 1
    outer = seq // inner
    half = length // RADIX
    there, back = middle_tables(length)
    blocks = struct((seq, rows, own), BF16)
    spectrum = struct((half + 1, 2 * RADIX, 2 * own), F32)
    mid = pltpu.VMEM((half + 1, 2 * RADIX, 2 * own), BF16)
    work = 300 * (half + 1) * RADIX**2 * own
    start = (me * rows).astype(jnp.int32)[None]
    rates = decay[None, :]

    halves, full_grad = gather_columns(out_grad, "tp")
    (packed,) = call(
        functools.partial(pack_kernel, length=length),
        [struct((seq, 2, rows, own), BF16)],
        (values, filt, rates, start),
        scalar=(3,),
    )
    moved = exchange(packed)

    grad_y = jnp.dot(full_grad, out_weight, preferred_element_type=F32).astype(BF16)
    (gated_grad,) = call(gated_kernel, [struct((seq, 1, rows, own), BF16)], (grad_y, gate))
    gated_grad, moved = lax.optimization_barrier((gated_grad, moved))
    grad_c = exchange(gated_grad)

    place = (me % inner).astype(jnp.int32)[None]
    (gates,) = call(
        layer_pack_kernel, [struct((inner, outer, rows, own), BF16)], (gate, place), scalar=(1,)
    )
    gates, _ = lax.optimization_barrier((gates, moved))
    order, turned, across = layer_grads(halves, inner)
    if across:
        across[0], *turned, moved = lax.optimization_barrier((across[0], *turned, moved))
    spec, conv_out_c = call(
        conv_kernel,
        [spectrum, blocks],
        (moved, there, back),
        scratch=(mid,),
        flops=work,
    )
    if len(turned) == 2 and across:
        late, _ = lax.optimization_barrier((across[0], conv_out_c))
        across.append(swap(late, "tp", 2, 1))
    grads = [list(pair) for pair in (zip(turned, across) if across else zip(turned))]
    gates = [swap(gates[bit], "seq", seq, bit) if bit else gates[bit] for bit in order]
    conv_out_c, grad_c = lax.optimization_barrier((conv_out_c, grad_c))
    layers = [[z * inner + w for z in range(outer)] for w in range(inner)]
    conv_out = exchange(conv_out_c.reshape(outer, inner, rows, own), layers)

    *gates, grad_c = lax.optimization_barrier((*gates, grad_c))
    conv_grad, kernel_grad = call(
        grad_kernel,
        [blocks, struct((seq, rows + STEP, own), BF16)],
        (grad_c, moved, spec, there, back),
        scratch=(mid,),
        flops=work,
    )
    flat, gates, _ = lax.optimization_barrier((sum(grads, []), gates, conv_grad))
    count = len(flat) // len(grads)
    grads = [flat[i : i + count] for i in range(0, len(flat), count)]
    bit = inner // 4
    while bit:
        grads = [g + [swap(part, "seq", seq, bit) for part in g] for g in grads]
        bit //= 2
    conv_grad, conv_out = lax.optimization_barrier((conv_grad, conv_out))
    conv_grad = exchange(conv_grad)

    block = struct((rows, width), BF16)
    home = struct((outer, rows, own), BF16)
    gated_out, *homes = call(
        functools.partial(layer_kernel, order=order),
        [struct((inner * rows, outer * own), BF16)] + [home] * inner,
        (*gates, conv_out, place),
        scalar=(inner + 1,),
    )
    shift = 0
    if len(grads) == 2:
        shift = lax.axis_index("tp") * (outer // 2)
    terms = [None] * outer
    for d in sorted(range(outer), key=lambda d: (-(d % 2), -d)):
        terms[d] = outer_product(grads, gated_out, (me // inner) ^ d ^ shift, outer)
        gated_out, _ = lax.optimization_barrier((gated_out, terms[d]))
    kernel_grad, conv_grad, _ = lax.optimization_barrier((kernel_grad, conv_grad, terms[1 % outer]))
    kernel_grad = exchange(kernel_grad)

    homes = {bit: swap(part, "seq", seq, bit) if bit else part for bit, part in zip(order, homes)}
    homes = jnp.stack([homes[bit] for bit in range(inner)])
    (d_gate,) = call(gate_kernel, [block], (homes, grad_y, place), scalar=(2,))
    chunks = 1
    wide = outer * own // chunks
    totals, conv_grad, kernel_grad = halving_reduce_scatter(
        terms, seq, inner, chunks, conv_grad, kernel_grad
    )
    (d_values,) = call(values_kernel, [block], (conv_grad,))
    d_filt, decay_grad = call(
        functools.partial(filt_kernel, length=length),
        [struct((rows, width), F32), struct((1, width), F32)],
        (kernel_grad, rates, start),
        scalar=(2,),
    )
    totals[-1], d_gate, d_values = lax.optimization_barrier((totals[-1], d_gate, d_values))
    pieces = []
    for total in totals:
        total = total.astype(BF16).reshape(inner, -1, wide)
        for bit in range(inner):
            piece = lax.dynamic_index_in_dim(total, (me % inner) ^ bit, 0, keepdims=False)
            pieces.append(swap(piece, "seq", seq, bit) if bit else piece)
    pieces = jnp.stack(pieces).reshape(chunks, inner, -1, wide)
    (d_out_weight,) = call(
        functools.partial(weight_kernel, scale=norm_scale, own=own),
        [struct((pieces.shape[2], width), F32)],
        (pieces, place),
        scalar=(1,),
    )
    return (d_values, d_gate, d_filt, decay_grad[0], d_out_weight)


def solution(mesh):
    in_specs = (
        P("seq", "tp"),
        P("seq", "tp"),
        P("seq", "tp"),
        P(None, "tp"),
        P("seq", "tp"),
        P("tp"),
    )
    out_specs = (P("seq", "tp"), P("seq", "tp"), P("seq", "tp"), P("tp"), P("seq", "tp"))
    return jax.shard_map(
        on_device, mesh=mesh, in_specs=in_specs, out_specs=out_specs, check_vma=False
    )
```
